256 devices in a mesh: dp: 128 (over y, x, z), proto: 2 (over core).
Axes of the slice: x: 4, y: 4, z: 8, core: 2. Of those that a mesh axis runs over, the one named last changes fastest.
Arguments:
- teacher_feats: bfloat16 [1536, 2, 256], P('dp'), may hold values from -3 to 3
- student_feats: bfloat16 [1536, 10, 256], P('dp'), may hold values from -1 to 1
- proto_v: bfloat16 [256, 65536], P(None, ('dp', 'proto')), may hold values from -1 to 1
Outputs:
- row_loss: float32 [1536, 10], P('dp')
- grad_student: float32 [1536, 10, 256], P('dp')
- grad_v: float32 [256, 65536], P(None, ('dp', 'proto'))
The draws below stay inside these ranges and needn't reach their ends.
All inputs are finite; a program needn't handle non-finite values.
Results may differ from the reference program's by a relative error of at most 0.0022.
Values may be sent and summed in bfloat16 or wider, within the bound.
A program may use at most 192 MiB of HBM per device.

```python
import math
import jax
import jax.numpy as jnp
from jax import lax

D = 256
PROTOS = 65536
CROPS = 10
TEACH = 2
SWEEPS = 3
IMG_DEV = 12
IMAGES = 1536
N_DP = 128


def shared_parts(key):
    base_key = jax.random.fold_in(key, 977)
    direction_key, image_key = jax.random.split(base_key)
    directions = jax.random.truncated_normal(direction_key, -4.0, 4.0, (D, D), jnp.float32) / math.sqrt(D)
    cluster = jax.random.randint(image_key, (IMAGES,), 0, D)
    return (directions, cluster)


def draw_teacher_feats(key, part):
    directions, cluster = shared_parts(key)
    key = jax.random.fold_in(key, 11)
    noise_key = jax.random.fold_in(key, 0)
    signal = jnp.take(directions, cluster, axis=1).T[:, None, :]
    noise_part = jax.random.truncated_normal(noise_key, -4.0, 4.0, (IMAGES, TEACH, D), jnp.float32)
    features = signal + 0.8 * noise_part / math.sqrt(D)
    return features.astype(jnp.bfloat16)


def draw_student_feats(key, part):
    directions, cluster = shared_parts(key)
    key = jax.random.fold_in(key, 23)
    noise_key, scale_key = jax.random.split(key)
    signal = jnp.take(directions, cluster, axis=1).T[:, None, :]
    noise_part = jax.random.truncated_normal(noise_key, -4.0, 4.0, (IMAGES, CROPS, D), jnp.float32)
    row_scale = jnp.exp(jax.random.uniform(scale_key, (IMAGES, CROPS, 1), jnp.float32, math.log(0.05), math.log(0.5)))
    return ((signal + noise_part / math.sqrt(D)) * row_scale).astype(jnp.bfloat16)


def draw_proto_v(key, part):
    directions, cluster = shared_parts(key)
    key = jax.random.fold_in(key, 37)
    assign_key, noise_key, scale_key = jax.random.split(key, 3)
    assign = jax.random.randint(assign_key, (PROTOS,), 0, D)
    base_part = jnp.take(directions, assign, axis=1)
    noise_part = jax.random.truncated_normal(noise_key, -4.0, 4.0, (D, PROTOS), jnp.float32)
    column_scale = jnp.exp(jax.random.uniform(scale_key, (1, PROTOS), jnp.float32, math.log(0.01), math.log(0.1)))
    return ((base_part + noise_part / math.sqrt(D)) * column_scale).astype(jnp.bfloat16)


def setup_inputs(seed: int = 0) -> dict:
    key_list = jax.random.split(jax.random.key(seed), 4)
    return {
        "teacher_feats": draw_teacher_feats(jax.random.fold_in(key_list[3], 71), 0),
        "student_feats": draw_student_feats(jax.random.fold_in(key_list[3], 71), 0),
        "proto_v": draw_proto_v(jax.random.fold_in(key_list[3], 71), 0),
    }


epsilon = 1e-12
teacher_temp = 0.07
student_temp = 0.1

def targets_mix(targets, crop_count):
    first_crop = targets[:, 0]
    second_crop = targets[:, 1]
    average = (first_crop + second_crop) * 0.5
    locals_part = jnp.broadcast_to(average[:, None, :], (average.shape[0], crop_count - 2, average.shape[1]))
    return jnp.concatenate([second_crop[:, None, :], first_crop[:, None, :], locals_part], axis=1)

def reference(teacher_feats, student_feats, proto_v):
    proto_f = proto_v.astype(jnp.float32)
    colnorm = jnp.sqrt(lax.optimization_barrier(jnp.sum(proto_f * proto_f, axis=0, keepdims=True)) + epsilon)
    weight_f = proto_f / colnorm
    weight_b = weight_f.astype(jnp.bfloat16)
    teacher_f = teacher_feats.reshape(IMAGES * TEACH, D).astype(jnp.float32)
    teacher_n = (teacher_f / jnp.sqrt(lax.optimization_barrier(jnp.sum(teacher_f * teacher_f, axis=1, keepdims=True)) + epsilon)).astype(jnp.bfloat16)
    targets = jnp.exp(jnp.dot(teacher_n, weight_b, preferred_element_type=jnp.float32) / teacher_temp)
    for sweep_index in range(SWEEPS):
        targets = targets / lax.optimization_barrier(jnp.sum(targets, axis=0, keepdims=True))
        targets = targets / lax.optimization_barrier(jnp.sum(targets, axis=1, keepdims=True))
    targets = targets.reshape(N_DP, IMG_DEV, TEACH, PROTOS)
    students = student_feats.reshape(N_DP, IMG_DEV, CROPS, D)

    def scan_block(grad_w, block_pair):
        features, block_targets = block_pair
        student_raw = features.astype(jnp.float32)
        snorm = jnp.sqrt(lax.optimization_barrier(jnp.sum(student_raw * student_raw, axis=-1, keepdims=True)) + epsilon)
        student_f = student_raw / snorm
        student_b = student_f.astype(jnp.bfloat16).reshape(IMG_DEV * CROPS, D)
        logits = jnp.dot(student_b, weight_b, preferred_element_type=jnp.float32) / student_temp
        logits = logits.reshape(IMG_DEV, CROPS, PROTOS)
        exponent = jnp.exp(logits)
        zsum = lax.optimization_barrier(jnp.sum(exponent, axis=-1, keepdims=True))
        prob = exponent / zsum
        logp = logits - jnp.log(zsum)
        mixed = targets_mix(block_targets, CROPS)
        block_loss = -lax.optimization_barrier(jnp.sum(mixed * logp, axis=-1))
        dlogit = ((prob - mixed) / student_temp).astype(jnp.bfloat16).reshape(IMG_DEV * CROPS, PROTOS)
        grad_w = grad_w + lax.dot_general(student_b, dlogit, (((0,), (0,)), ((), ())), preferred_element_type=jnp.float32)
        grad_n = lax.dot_general(dlogit, weight_b, (((1,), (1,)), ((), ())), preferred_element_type=jnp.float32)
        grad_n = grad_n.reshape(IMG_DEV, CROPS, D)
        grad_rows = (grad_n - student_f * lax.optimization_barrier(jnp.sum(student_f * grad_n, axis=-1, keepdims=True))) / snorm
        return (grad_w, (block_loss, grad_rows))
    grad_w, (block_loss, grad_rows) = lax.scan(scan_block, jnp.zeros((D, PROTOS), jnp.float32), (students, targets))
    grad_v = (grad_w - weight_f * lax.optimization_barrier(jnp.sum(weight_f * grad_w, axis=0, keepdims=True))) / colnorm
    return (block_loss.reshape(IMAGES, CROPS), grad_rows.reshape(IMAGES, CROPS, D), grad_v)
```

```python
import math

import jax
import jax.numpy as jnp
import numpy as np
from jax import lax
from jax.experimental import pallas as pl
from jax.experimental.pallas import tpu as pltpu
from jax.sharding import PartitionSpec as P

MESH = pl.DeviceIdType.MESH
F32, BF16 = jnp.float32, jnp.bfloat16

epsilon = 1e-12
teacher_temp = 0.07
student_temp = 0.1
LOG2E = math.log2(math.e)

NY, NB, NA = 4, 32, 8
D = 256
PB = 256
SB, TB = 64, 16
SROWS, TROWS = SB * NB, TB * NB
IMG, CROPS, TEACH = 6, 10, 2
SWEEPS = 3
ST = 512
OUTW = D + 128


def mixing():
    m = np.zeros((SB, TB), np.float32)
    for img in range(IMG):
        for crop in range(CROPS):
            row, first = img * CROPS + crop, img * TEACH
            if crop == 0:
                m[row, first + 1] = 1.0
            elif crop == 1:
                m[row, first] = 1.0
            else:
                m[row, first] = m[row, first + 1] = 0.5
    return m


def dot(x, y, dims=((1,), (0,)), precision=None):
    return lax.dot_general(x, y, (dims, ((), ())), preferred_element_type=F32, precision=precision)


def wait_bytes(ref, sem):
    pltpu.make_async_copy(ref, ref, sem).wait()


def column(row):
    return jnp.broadcast_to(row, (128, 128)).T


def kernel(t_ref, s_ref, p_ref, mix_big_ref, mix_ref, out_ref, gv_ref,
           wg, tg, sg, k3, kv, e3, st_ref, szt, ub, gb, gr, hb, hr, gw, cs, cr, ys, yr,
           colbuf, rowbuf, zbuf, ztmp,
           w_ss, w_rs, t_ss, t_rs, s_ss, s_rs, col_ss, col_rs, row_ss, row_rs, z_ss, z_rs,
           g_ss, g_rs, h_ss, h_rs, c_ss, c_rs, y_ss, y_rs, o_ss, o_rs):
    dp = lax.axis_index("dp")
    c = lax.axis_index("proto")
    y, b = dp // NB, dp % NB
    a = y * 2 + c

    def a_dev(a2):
        return ((a2 // 2) * NB + b, a2 % 2)

    def b_dev(b2):
        return (y * NB + b2, c)

    def a_peer(o):
        return (a + o) % NA

    def b_peer(o):
        return (b + o) % NB

    def rows(i, n):
        return pl.ds(pl.multiple_of(i * n, n), n)

    def remote(src, dst, ss, rs, device):
        return pltpu.make_async_remote_copy(
            src_ref=src, dst_ref=dst, send_sem=ss, recv_sem=rs, device_id=device, device_id_type=MESH
        )

    barrier = pltpu.get_barrier_semaphore()

    @pl.loop(1, NA)
    def _(o):
        pl.semaphore_signal(barrier, inc=1, device_id=a_dev(a_peer(o)), device_id_type=MESH)

    @pl.loop(1, NB)
    def _(o):
        pl.semaphore_signal(barrier, inc=1, device_id=b_dev(b_peer(o)), device_id_type=MESH)

    proto_f = p_ref[...].astype(F32)
    colnorm = jnp.sqrt(jnp.sum(proto_f * proto_f, axis=0, keepdims=True) + epsilon)
    wg[a] = (proto_f / colnorm).astype(BF16)
    t_f = t_ref[...].astype(F32)
    tg[rows(b, TB), :] = (
        t_f / jnp.sqrt(jnp.sum(t_f * t_f, axis=1, keepdims=True) + epsilon)
    ).astype(BF16)
    s_raw = s_ref[...].astype(F32)
    snorm = jnp.sqrt(jnp.sum(s_raw * s_raw, axis=1, keepdims=True) + epsilon)
    sg[rows(b, SB), :] = (s_raw / snorm).astype(BF16)

    pl.semaphore_wait(barrier, NA - 1 + NB - 1)

    w_copies = []
    for o in range(1, NY):
        cp = remote(wg.at[a], wg.at[a], w_ss.at[o - 1], w_rs.at[a], a_dev(a_peer(2 * o)))
        cp.start()
        w_copies.append(cp)

    def b_all(src, dst, ss, rs):
        @pl.loop(1, NB)
        def _(o):
            remote(src(b_peer(o)), dst, ss, rs, b_dev(b_peer(o))).start()

    t_own = tg.at[rows(b, TB), :]
    b_all(lambda _: t_own, t_own, t_ss, t_rs)
    cp = remote(wg.at[a], wg.at[a], w_ss.at[NY - 1], w_rs.at[a], (dp, 1 - c))
    cp.start()
    w_copies.append(cp)
    s_own = sg.at[rows(b, SB), :]
    b_all(lambda _: s_own, s_own, s_ss, s_rs)

    for o in range(1, NY):
        a2 = a_peer(2 * (NY - o))
        wait_bytes(wg.at[a2], w_rs.at[a2])
        cp = remote(wg.at[a2], wg.at[a2], w_ss.at[NY - 1 + o], w_rs.at[a2], (dp, 1 - c))
        cp.start()
        w_copies.append(cp)
    for y2 in range(NY):
        a2 = y2 * 2 + 1 - c
        wait_bytes(wg.at[a2], w_rs.at[a2])
    wait_bytes(tg.at[pl.ds(0, (NB - 1) * TB), :], t_rs)

    valid = (lax.broadcasted_iota(jnp.int32, (1, TROWS), 1) % TB < IMG * TEACH).astype(F32)

    def set_u(u_row):
        for r in range(TROWS // 128):
            ub[r * 128:(r + 1) * 128, :] = column(u_row[:, r * 128:(r + 1) * 128])

    set_u(valid)

    def col_send(sweep):
        src = colbuf.at[sweep, a]

        @pl.loop(1, NA)
        def _(o):
            remote(src, src, col_ss.at[sweep], col_rs.at[sweep], a_dev(a_peer(o))).start()

    def col_wait(sweep):
        wait_bytes(colbuf.at[sweep, pl.ds(0, NA - 1)], col_rs.at[sweep])
        total = colbuf[sweep, 0]
        for i in range(1, NA):
            total = total + colbuf[sweep, i]
        return 1.0 / total

    def row_send(sweep):
        src = rowbuf.at[sweep, b]
        b_all(lambda _: src, src, row_ss.at[sweep], row_rs.at[sweep])

    def row_wait(sweep):
        wait_bytes(rowbuf.at[sweep, pl.ds(0, NB - 1)], row_rs.at[sweep])
        total = rowbuf[sweep, 0]
        for i in range(1, NB):
            total = total + rowbuf[sweep, i]
        return valid / total

    def col_part(sweep):
        @pl.loop(0, NA)
        def _(i):
            u2 = ub[...]
            part = jnp.sum(k3[i] * jnp.concatenate([u2, u2], axis=1), axis=0, keepdims=True)
            colbuf[sweep, a, :, rows(i, PB)] = part

    def row_part(sweep, v, last):
        @pl.loop(0, TROWS // 128)
        def _(r):
            acc = jnp.zeros((128, 128), F32)
            h = jnp.zeros((128, D), F32)
            for i in range(NA):
                scaled = k3[i, rows(r, 128), :] * v[:, i * PB:(i + 1) * PB]
                acc = acc + scaled[:, :128] + scaled[:, 128:]
                if last:
                    scaled = scaled.astype(BF16)
                    kv[i, rows(r, 128), :] = scaled
                    h = h + dot(scaled, wg[i], ((1,), (1,)))
            rowbuf[sweep, b, :, rows(r, 128)] = jnp.sum(acc.T, axis=0, keepdims=True)
            if last:
                hb[rows(r, 128), :] = h.astype(BF16)

    @pl.loop(0, NA)
    def _(i):
        k3[i] = jnp.exp2(dot(tg[...], wg[i]) * (LOG2E / teacher_temp))

    def student(step):
        @pl.loop(step, step + 1)
        def _(r):
            x = sg[rows(r, ST), :]
            z = jnp.zeros((ST, 128), F32)
            g = jnp.zeros((ST, D), F32)
            for i in range(NA):
                e = jnp.exp2(dot(x, wg[i]) * (LOG2E / student_temp))
                z = z + e[:, :128] + e[:, 128:]
                e = e.astype(BF16)
                e3[i, rows(r, ST), :] = e
                g = g + dot(e, wg[i], ((1,), (1,)))
            gb[rows(r, ST), :] = g.astype(BF16)
            for j in range(ST // 128):
                part = jnp.sum(z[j * 128:(j + 1) * 128, :].T, axis=0, keepdims=True)
                zbuf[b, :, pl.ds(pl.multiple_of(r * ST, ST) + j * 128, 128)] = part
                x_t = x[j * 128:(j + 1) * 128, :].astype(F32).T
                st_ref[:, pl.ds(pl.multiple_of(r * ST, ST) + j * 128, 128)] = x_t.astype(BF16)

    col_part(0)
    col_send(0)
    v = col_wait(0)
    row_part(0, v, False)
    row_send(0)
    set_u(row_wait(0))
    col_part(1)
    col_send(1)
    v = col_wait(1)
    row_part(1, v, False)
    row_send(1)
    wait_bytes(sg.at[pl.ds(0, (NB - 1) * SB), :], s_rs)
    steps = SROWS // ST
    for step in range(steps // 2):
        student(step)
    set_u(row_wait(1))
    col_part(2)
    col_send(2)
    for step in range(steps // 2, steps):
        student(step)
    z_src = zbuf.at[b]
    b_all(lambda _: z_src, z_src, z_ss, z_rs)
    v = col_wait(2)
    row_part(2, v, True)
    row_send(2)
    b_all(lambda b2: hb.at[rows(b2, TB), :], hr.at[b], h_ss, h_rs)
    b_all(lambda b2: gb.at[rows(b2, SB), :], gr.at[b], g_ss, g_rs)

    wait_bytes(zbuf.at[pl.ds(0, NB - 1)], z_rs)
    zsum = zbuf[0]
    for i in range(1, NB):
        zsum = zsum + zbuf[i]
    ztmp[...] = zsum
    z_inv = 1.0 / zsum
    for j in range(SROWS // 512):
        szt[:, j * 512:(j + 1) * 512] = (
            st_ref[:, j * 512:(j + 1) * 512].astype(F32) * z_inv[:, j * 512:(j + 1) * 512]
        ).astype(BF16)

    @pl.loop(0, NA)
    def _(i):
        gw[i] = dot(szt[...], e3[i])

    u_row = row_wait(2)
    set_u(u_row)
    ua = []
    for j in range(TROWS // 128):
        mixed_t = dot(st_ref[:, j * 512:(j + 1) * 512], mix_big_ref[...])
        ua.append(mixed_t * u_row[:, j * 128:(j + 1) * 128])
    ua = jnp.concatenate(ua, axis=1)
    ua_high = ua.astype(BF16)
    ua = jnp.concatenate([ua_high, (ua - ua_high.astype(F32)).astype(BF16)], axis=0)

    def teacher_part(i):
        both = dot(ua, kv[i])
        return both[:D] + both[D:]

    for y2 in range(NY):
        i = y2 * 2 + 1 - c
        cs[y2] = gw[i] - teacher_part(i)
        remote(cs.at[y2], cr.at[y2], c_ss.at[y2], c_rs.at[y2], (dp, 1 - c)).start()
    for y2 in range(NY):
        i = y2 * 2 + c
        gw[i] = gw[i] - teacher_part(i)
    for o in list(range(1, NY)) + [0]:
        y2 = (y + o) % NY
        i = y2 * 2 + c
        wait_bytes(cr.at[y2], c_rs.at[y2])
        both = gw[i] + cr[y2]
        if o:
            ys[o - 1] = both.astype(BF16)
            remote(ys.at[o - 1], yr.at[o - 1], y_ss.at[o - 1], y_rs.at[o - 1],
                   (y2 * NB + b, c)).start()
        else:
            gw[i] = both

    hr[b] = hb[rows(b, TB), :]
    gr[b] = gb[rows(b, SB), :]
    wait_bytes(hr.at[pl.ds(0, NB - 1)], h_rs)
    h = jnp.zeros((TB, D), F32)
    for i in range(NB):
        h = h + hr[i].astype(F32)
    u_own = ub[rows(b, TB), :]
    mixed = dot(mix_ref[...], h * jnp.concatenate([u_own, u_own], axis=1),
                precision=lax.Precision.HIGHEST)
    wait_bytes(gr.at[pl.ds(0, NB - 1)], g_rs)
    g = lax.fori_loop(0, NB, lambda i, t: t + gr[i].astype(F32), jnp.zeros((SB, D), F32))
    ub[0:128, :] = column(ztmp[:, rows(b // 2, 128)])
    z_own = ub[rows(b % 2, SB), :]
    student_f = s_raw / snorm
    student_b = student_f.astype(BF16).astype(F32)
    grad_n = (g / jnp.concatenate([z_own, z_own], axis=1) - mixed) / student_temp
    loss = jnp.log(z_own) - jnp.sum(student_b * mixed, axis=1, keepdims=True) / student_temp
    grad_s = (grad_n - student_f * jnp.sum(student_f * grad_n, axis=1, keepdims=True)) / snorm
    out_ref[c, :, 0:D] = grad_s
    out_ref[c, :, D:] = loss
    out_copy = remote(out_ref.at[c], out_ref.at[c], o_ss, o_rs, (dp, 1 - c))
    out_copy.start()

    grad_w = gw[a]
    for o in range(1, NY):
        wait_bytes(yr.at[o - 1], y_rs.at[o - 1])
        grad_w = grad_w + yr[o - 1].astype(F32)
    grad_w = grad_w / student_temp
    weight_f = proto_f / colnorm
    gv_ref[...] = (
        grad_w - weight_f * jnp.sum(weight_f * grad_w, axis=0, keepdims=True)
    ) / colnorm

    wait_bytes(out_ref.at[1 - c], o_rs)
    out_copy.wait_send()
    for cp in w_copies:
        cp.wait_send()
    wait_bytes(tg.at[pl.ds(0, (NB - 1) * TB), :], t_ss)
    wait_bytes(sg.at[pl.ds(0, (NB - 1) * SB), :], s_ss)
    for sweep in range(SWEEPS):
        wait_bytes(colbuf.at[sweep, pl.ds(0, NA - 1)], col_ss.at[sweep])
        wait_bytes(rowbuf.at[sweep, pl.ds(0, NB - 1)], row_ss.at[sweep])
    wait_bytes(zbuf.at[pl.ds(0, NB - 1)], z_ss)
    wait_bytes(gr.at[pl.ds(0, NB - 1)], g_ss)
    wait_bytes(hr.at[pl.ds(0, NB - 1)], h_ss)
    for y2 in range(NY):
        wait_bytes(cs.at[y2], c_ss.at[y2])
    for o in range(1, NY):
        wait_bytes(ys.at[o - 1], y_ss.at[o - 1])


def shards(teacher_feats, student_feats, proto_v):
    c = lax.axis_index("proto")
    t = lax.dynamic_slice_in_dim(teacher_feats, c * IMG, IMG, 0).reshape(IMG * TEACH, D)
    s = lax.dynamic_slice_in_dim(student_feats, c * IMG, IMG, 0).reshape(IMG * CROPS, D)
    t = jnp.pad(t, ((0, TB - IMG * TEACH), (0, 0)))
    s = jnp.pad(s, ((0, SB - IMG * CROPS), (0, 0)))
    mix = mixing()
    mix_big = jnp.asarray(np.kron(np.eye(8, dtype=np.float32), mix), BF16)
    vmem = pl.BlockSpec(memory_space=pltpu.VMEM)
    dma = pltpu.SemaphoreType.DMA
    out, grad_v = pl.pallas_call(
        kernel,
        out_shape=(
            jax.ShapeDtypeStruct((2, SB, OUTW), F32),
            jax.ShapeDtypeStruct((D, PB), F32),
        ),
        in_specs=[vmem] * 5,
        out_specs=(vmem, vmem),
        scratch_shapes=[
            pltpu.VMEM((NA, D, PB), BF16),
            pltpu.VMEM((TROWS, D), BF16),
            pltpu.VMEM((SROWS, D), BF16),
            pltpu.VMEM((NA, TROWS, PB), F32),
            pltpu.VMEM((NA, TROWS, PB), BF16),
            pltpu.VMEM((NA, SROWS, PB), BF16),
            pltpu.VMEM((D, SROWS), BF16),
            pltpu.VMEM((D, SROWS), BF16),
            pltpu.VMEM((TROWS, 128), F32),
            pltpu.VMEM((SROWS, D), BF16),
            pltpu.VMEM((NB, SB, D), BF16),
            pltpu.VMEM((TROWS, D), BF16),
            pltpu.VMEM((NB, TB, D), BF16),
            pltpu.VMEM((NA, D, PB), F32),
            pltpu.VMEM((NY, D, PB), F32),
            pltpu.VMEM((NY, D, PB), F32),
            pltpu.VMEM((NY - 1, D, PB), BF16),
            pltpu.VMEM((NY - 1, D, PB), BF16),
            pltpu.VMEM((SWEEPS, NA, 1, NA * PB), F32),
            pltpu.VMEM((SWEEPS, NB, 1, TROWS), F32),
            pltpu.VMEM((NB, 1, SROWS), F32),
            pltpu.VMEM((1, SROWS), F32),
            dma((2 * NY - 1,)), dma((NA,)),
            dma, dma, dma, dma,
            dma((SWEEPS,)), dma((SWEEPS,)), dma((SWEEPS,)), dma((SWEEPS,)),
            dma, dma, dma, dma, dma, dma,
            dma((NY,)), dma((NY,)),
            dma((NY - 1,)), dma((NY - 1,)),
            dma, dma,
        ],
        compiler_params=pltpu.CompilerParams(
            collective_id=0, has_side_effects=True, vmem_limit_bytes=56 << 20
        ),
        name="head_step",
    )(t, s, proto_v, mix_big, jnp.asarray(mix))
    out = out[:, : IMG * CROPS, :].reshape(2 * IMG, CROPS, OUTW)
    return (out[:, :, D], out[:, :, :D], grad_v)


def solution(mesh):
    in_specs = (P("dp", None, None), P("dp", None, None), P(None, ("dp", "proto")))
    out_specs = (P("dp", None), P("dp", None, None), P(None, ("dp", "proto")))
    return jax.shard_map(shards, mesh=mesh, in_specs=in_specs, out_specs=out_specs, check_vma=False)
```

```python
import math

import jax
import jax.numpy as jnp
import numpy as np
from jax import lax
from jax.experimental import pallas as pl
from jax.experimental.pallas import tpu as pltpu
from jax.sharding import PartitionSpec as P

MESH = pl.DeviceIdType.MESH
F32, BF16 = jnp.float32, jnp.bfloat16

epsilon = 1e-12
teacher_temp = 0.07
student_temp = 0.1
LOG2E = math.log2(math.e)

NY, NX, NZ = 4, 4, 8
NB, NA = NX * NZ, NY * 2
D = 256
PB = 256
SB, TB = 64, 16
SROWS, TROWS = SB * NB, TB * NB
IMG, CROPS, TEACH = 6, 10, 2
SWEEPS = 3
ST = SB * NZ
OUTW = D + 128


def mixing():
    m = np.zeros((SB, TB), np.float32)
    for img in range(IMG):
        for crop in range(CROPS):
            row, first = crop * IMG + img, img * TEACH
            if crop == 0:
                m[row, first + 1] = 1.0
            elif crop == 1:
                m[row, first] = 1.0
            else:
                m[row, first] = m[row, first + 1] = 0.5
    return m


def dot(x, y, dims=((1,), (0,)), precision=None):
    return lax.dot_general(x, y, (dims, ((), ())), preferred_element_type=F32, precision=precision)


def wait_bytes(ref, sem):
    pltpu.make_async_copy(ref, ref, sem).wait()


def column(row):
    return jnp.broadcast_to(row, (128, 128)).T


def kernel(t_ref, s_ref, p_ref, mix_big_ref, mix_ref, out_ref, gv_ref,
           wg, tg, sg, k3, kv, e3, st_ref, szt, ub, gb, gs, gx, gz, gr, hb, hx, hz, hr, gw, cs, cr, ys, yr,
           colbuf, rowbuf, zx, zbuf, zown, ztmp, ztot, traw, sraw, at, ats, kvs, uu,
           w_ss, w_rs, t_ss, t_rs, sz_ss, sz_rs, sx_ss, sx_rs, gx_ss, gx_rs, col_ss, col_rs, row_ss, row_rs, z_ss, z_rs,
           g_ss, g_rs, h_ss, h_rs, c_ss, c_rs, y_ss, y_rs, o_ss, o_rs,
           k_ss, k_rs, at_ss, at_rs, u_ss, u_rs, zx_ss, zx_rs, hx_ss, hx_rs):
    dp = lax.axis_index("dp")
    c = lax.axis_index("proto")
    y, b = dp // NB, dp % NB
    x, zz = b // NZ, b % NZ
    a = y * 2 + c

    def a_dev(a2):
        return ((a2 // 2) * NB + b, a2 % 2)

    def b_dev(b2):
        return (y * NB + b2, c)

    def a_peer(o):
        return (a + o) % NA

    def x_peer(o):
        return (x + o) % NX

    def z_peer(o):
        return (zz + o) % NZ

    def far(i, n):
        return (n // 2 + (2 * (i % 2) - 1) * ((i + 1) // 2)) % n

    def b_far(i):
        return x_peer(far(i % NX, NX)) * NZ + z_peer(far(i // NX, NZ))

    def rows(i, n):
        return pl.ds(pl.multiple_of(i * n, n), n)

    def remote(src, dst, ss, rs, device):
        return pltpu.make_async_remote_copy(
            src_ref=src, dst_ref=dst, send_sem=ss, recv_sem=rs, device_id=device, device_id_type=MESH
        )

    comms = {
        "t": (tg.at[pl.ds(0, (NB - 1) * TB), :], t_ss, t_rs),
        "at": (at, at_ss, at_rs),
        "u": (uu.at[0], u_ss, u_rs),
        "zx": (zx, zx_ss, zx_rs),
        "z": (zbuf, z_ss, z_rs),
        "hx": (hx, hx_ss, hx_rs),
        "g": (gr.at[pl.ds(0, NZ - 1)], g_ss, g_rs),
        "h": (hr, h_ss, h_rs),
    }
    for sweep in range(SWEEPS):
        comms["col%d" % sweep] = (colbuf.at[sweep, pl.ds(0, NA - 1)], col_ss.at[sweep], col_rs.at[sweep])
        comms["row%d" % sweep] = (rowbuf.at[sweep, pl.ds(0, NB - 1)], row_ss.at[sweep], row_rs.at[sweep])
    for z2 in range(1, NZ):
        comms["sz%d" % z2] = (sg.at[pl.ds(0, SB), :], sz_ss.at[z2 - 1], sz_rs.at[z2 - 1])
    for o in range(1, NX):
        comms["sx%d" % o] = (sg.at[pl.ds(0, NZ * SB), :], sx_ss.at[o - 1], sx_rs.at[o - 1])
        comms["gx%d" % o] = (gx.at[o - 1], gx_ss.at[o - 1], gx_rs.at[o - 1])
    for y2 in range(NY):
        comms["c%d" % y2] = (cs.at[y2], c_ss.at[y2], c_rs.at[y2])
        comms["k%d" % y2] = (kvs.at[y2], k_ss.at[y2], k_rs.at[y2])
    for o in range(NY - 1):
        comms["y%d" % o] = (ys.at[o], y_ss.at[o], y_rs.at[o])
    started, received = [], set()

    def recv(name):
        wait_bytes(comms[name][0], comms[name][2])
        received.add(name)

    def finish():
        for name in started:
            if name not in received:
                recv(name)
            wait_bytes(comms[name][0], comms[name][1])
        for cp in w_copies:
            cp.wait_send()

    barrier = pltpu.get_barrier_semaphore()

    @pl.loop(0, NB - 1)
    def _(i):
        pl.semaphore_signal(barrier, inc=1, device_id=b_dev(b_far(i)), device_id_type=MESH)

    @pl.loop(1, NA)
    def _(o):
        pl.semaphore_signal(barrier, inc=1, device_id=a_dev(a_peer(o)), device_id_type=MESH)

    proto_f = p_ref[...].astype(F32)
    colnorm = jnp.sqrt(jnp.sum(proto_f * proto_f, axis=0, keepdims=True) + epsilon)
    wg[a] = (proto_f / colnorm).astype(BF16)
    traw[...] = jnp.zeros_like(traw)
    for img in range(IMG):
        traw[img * TEACH:(img + 1) * TEACH, :] = t_ref[c * IMG + img].astype(F32)
    t_f = traw[...]
    tg[rows(b, TB), :] = (
        t_f / jnp.sqrt(jnp.sum(t_f * t_f, axis=1, keepdims=True) + epsilon)
    ).astype(BF16)
    sraw[...] = jnp.zeros_like(sraw)
    for crop in range(CROPS):
        both = s_ref[crop].astype(F32)
        sraw[crop * IMG:(crop + 1) * IMG, :] = jnp.where(c == 0, both[:IMG], both[IMG:])
    s_raw = sraw[...]
    snorm = jnp.sqrt(jnp.sum(s_raw * s_raw, axis=1, keepdims=True) + epsilon)
    sg[rows(b, SB), :] = (s_raw / snorm).astype(BF16)

    pl.semaphore_wait(barrier, NA - 1 + NB - 1)

    w_copies = []
    for o in (2, 1, 3):
        cp = remote(wg.at[a], wg.at[a], w_ss.at[o - 1], w_rs.at[a], a_dev(a_peer(2 * o)))
        cp.start()
        w_copies.append(cp)

    def b_all(name, src, dst):
        started.append(name)
        _, ss, rs = comms[name]

        @pl.loop(0, NB - 1)
        def _(i):
            b2 = b_far(i)
            remote(src(b2), dst, ss, rs, b_dev(b2)).start()

    def to_sibling(name, src, dst):
        started.append(name)
        remote(src, dst, comms[name][1], comms[name][2], (dp, 1 - c)).start()

    t_own = tg.at[rows(b, TB), :]
    b_all("t", lambda _: t_own, t_own)
    cp = remote(wg.at[a], wg.at[a], w_ss.at[NY - 1], w_rs.at[a], (dp, 1 - c))
    cp.start()
    w_copies.append(cp)
    s_own = sg.at[rows(b, SB), :]

    def s_forward(z2):
        src = sg.at[rows(x * NZ + z2, SB), :]
        for o in range(1, NX):
            remote(src, src, sx_ss.at[o - 1], sx_rs.at[o - 1], b_dev(x_peer(o) * NZ + zz)).start()

    z_order = [1, 7, 2, 6, 3, 5, 4]
    for o in z_order:
        started.append("sz%d" % o)
        remote(s_own, s_own, sz_ss.at[o - 1], sz_rs.at[o - 1], b_dev(x * NZ + z_peer(o))).start()
    for o in range(1, NX):
        started.append("sx%d" % o)
    s_forward(zz)

    for o in range(1, NY):
        a2 = a_peer(2 * (NY - o))
        wait_bytes(wg.at[a2], w_rs.at[a2])
        cp = remote(wg.at[a2], wg.at[a2], w_ss.at[NY - 1 + o], w_rs.at[a2], (dp, 1 - c))
        cp.start()
        w_copies.append(cp)
    for o in (7, 1, 6, 2, 5, 3, 4):
        recv("sz%d" % o)
        s_forward(z_peer(NZ - o))
    for y2 in range(NY):
        a2 = y2 * 2 + 1 - c
        wait_bytes(wg.at[a2], w_rs.at[a2])
    recv("t")

    valid = (lax.broadcasted_iota(jnp.int32, (1, TROWS), 1) % TB < IMG * TEACH).astype(F32)

    def set_u(u_row):
        for r in range(TROWS // 128):
            ub[r * 128:(r + 1) * 128, :] = column(u_row[:, r * 128:(r + 1) * 128])

    set_u(valid)

    def col_send(sweep):
        src = colbuf.at[sweep, a]
        started.append("col%d" % sweep)

        @pl.loop(1, NA)
        def _(o):
            remote(src, src, col_ss.at[sweep], col_rs.at[sweep], a_dev(a_peer(o))).start()

    def col_wait(sweep):
        recv("col%d" % sweep)
        total = colbuf[sweep, 0]
        for i in range(1, NA):
            total = total + colbuf[sweep, i]
        return 1.0 / total

    def row_send(sweep):
        src = rowbuf.at[sweep, b]
        b_all("row%d" % sweep, lambda _: src, src)

    def row_wait(sweep):
        recv("row%d" % sweep)
        total = rowbuf[sweep, 0]
        for i in range(1, NB):
            total = total + rowbuf[sweep, i]
        return valid / total

    def col_part(sweep):
        @pl.loop(0, NA)
        def _(i):
            u2 = ub[...]
            part = jnp.sum(k3[i] * jnp.concatenate([u2, u2], axis=1), axis=0, keepdims=True)
            colbuf[sweep, a, :, rows(i, PB)] = part

    def row_part(sweep, v, last):
        @pl.loop(0, TROWS // 128)
        def _(r):
            acc = jnp.zeros((128, 128), F32)
            h = jnp.zeros((128, D), F32)
            for i in range(NA):
                scaled = k3[i, rows(r, 128), :] * v[:, i * PB:(i + 1) * PB]
                acc = acc + scaled[:, :128] + scaled[:, 128:]
                if last:
                    scaled = scaled.astype(BF16)
                    kv[i, rows(r, 128), :] = scaled
                    h = h + dot(scaled, wg[i], ((1,), (1,)))
            rowbuf[sweep, b, :, rows(r, 128)] = jnp.sum(acc.T, axis=0, keepdims=True)
            if last:
                hb[rows(r, 128), :] = h.astype(BF16)

    @pl.loop(0, NA)
    def _(i):
        k3[i] = jnp.exp2(dot(tg[...], wg[i]) * (LOG2E / teacher_temp))

    def student(step):
        @pl.loop(step, step + 1)
        def _(step):
            r = x_peer(NX - step)
            feats = sg[rows(r, ST), :]
            z = jnp.zeros((ST, 128), F32)
            g = jnp.zeros((ST, D), F32)
            for i in range(NA):
                e = jnp.exp2(dot(feats, wg[i]) * (LOG2E / student_temp))
                z = z + e[:, :128] + e[:, 128:]
                e = e.astype(BF16)
                e3[i, rows(r, ST), :] = e
                g = g + dot(e, wg[i], ((1,), (1,)))
            gb[step] = g
            for j in range(ST // 128):
                part = jnp.sum(z[j * 128:(j + 1) * 128, :].T, axis=0, keepdims=True)
                zown[:, pl.ds(pl.multiple_of(r * ST, ST) + j * 128, 128)] = part
                f_t = feats[j * 128:(j + 1) * 128, :].astype(F32).T
                st_ref[:, pl.ds(pl.multiple_of(r * ST, ST) + j * 128, 128)] = f_t.astype(BF16)

    def student_send(step):
        if step:
            o = NX - step
            gs[step - 1] = gb[step].astype(BF16)
            started.append("gx%d" % o)
            remote(gs.at[step - 1], gx.at[o - 1], gx_ss.at[o - 1], gx_rs.at[o - 1],
                   b_dev(x_peer(o) * NZ + zz)).start()

    def student_step(step):
        if step:
            recv("sx%d" % step)
        student(step)

    col_part(0)
    col_send(0)
    student_step(0)
    v = col_wait(0)
    row_part(0, v, False)
    row_send(0)
    student_step(1)
    student_step(3)
    set_u(row_wait(0))
    col_part(1)
    col_send(1)
    student_send(1)
    student_send(3)
    student_step(2)
    started.append("zx")
    for o in range(1, NX):
        remote(zown, zx.at[o - 1], zx_ss, zx_rs, b_dev(x_peer(o) * NZ + zz)).start()
    v = col_wait(1)
    row_part(1, v, False)
    row_send(1)
    recv("zx")
    ztmp[...] = zown[...] + zx[0] + zx[1] + zx[2]
    set_u(row_wait(1))
    col_part(2)
    col_send(2)
    student_send(2)
    started.append("z")
    for o in z_order:
        remote(ztmp, zbuf.at[o - 1], z_ss, z_rs, b_dev(x * NZ + z_peer(o))).start()
    for j in range(TROWS // 128):
        at[:, j * 128:(j + 1) * 128] = dot(st_ref[:, j * 512:(j + 1) * 512], mix_big_ref[...])
    to_sibling("at", at, ats)
    v = col_wait(2)
    row_part(2, v, True)
    row_send(2)
    started.append("hx")
    for o in range(1, NX):
        remote(hb.at[rows(x_peer(o), NZ * TB), :], hx.at[o - 1], hx_ss, hx_rs,
               b_dev(x_peer(o) * NZ + zz)).start()
    for y2 in range(NY):
        to_sibling("k%d" % y2, kv.at[y2 * 2 + 1 - c], kvs.at[y2])
    recv("z")
    zsum = ztmp[...]
    for i in range(NZ - 1):
        zsum = zsum + zbuf[i]
    ztot[...] = zsum
    z_inv = 1.0 / zsum
    for j in range(SROWS // 512):
        szt[:, j * 512:(j + 1) * 512] = (
            st_ref[:, j * 512:(j + 1) * 512].astype(F32) * z_inv[:, j * 512:(j + 1) * 512]
        ).astype(BF16)
    for y2 in range(NY):
        cs[y2] = dot(szt[...], e3[y2 * 2 + 1 - c])
        to_sibling("c%d" % y2, cs.at[y2], cr.at[y2])
    for y2 in range(NY):
        gw[y2] = dot(szt[...], e3[y2 * 2 + c])
    for o in range(1, NX):
        recv("gx%d" % o)
    started.append("g")
    for o in z_order + [0]:
        z2 = z_peer(o)
        g = gb[0, rows(z2, SB), :]
        for i in range(NX - 1):
            g = g + gx[i, rows(z2, SB), :].astype(F32)
        gz[o] = g.astype(BF16)
        if o:
            remote(gz.at[o], gr.at[o - 1], g_ss, g_rs, b_dev(x * NZ + z2)).start()
    u_row = row_wait(2)
    uu[c] = u_row
    to_sibling("u", uu.at[c], uu.at[c])
    recv("hx")
    started.append("h")
    for o in z_order + [0]:
        z2 = z_peer(o)
        h = hb[rows(x * NZ + z2, TB), :].astype(F32)
        for i in range(NX - 1):
            h = h + hx[i, rows(z2, TB), :].astype(F32)
        hz[o] = h.astype(BF16)
        if o:
            remote(hz.at[o], hr.at[o - 1], h_ss, h_rs, b_dev(x * NZ + z2)).start()
    set_u(u_row)

    def scaled_mix(mixed_t, u2):
        full = mixed_t * u2
        high = full.astype(BF16)
        return jnp.concatenate([high, (full - high.astype(F32)).astype(BF16)], axis=0)

    def teacher_part(ua, k2):
        both = dot(ua, k2)
        return both[:D] + both[D:]

    ua = scaled_mix(at[...], u_row)
    for y2 in range(NY):
        gw[y2] = gw[y2] - teacher_part(ua, kv[y2 * 2 + c])
    recv("at")
    recv("u")
    ua = scaled_mix(ats[...], uu[1 - c])
    for name in range(NY):
        recv("k%d" % name)
        recv("c%d" % name)
    for o in (2, 1, 3, 0):
        y2 = (y + o) % NY
        both = gw[y2] + cr[y2] - teacher_part(ua, kvs[y2])
        if o:
            ys[o - 1] = both.astype(BF16)
            started.append("y%d" % (o - 1))
            remote(ys.at[o - 1], yr.at[o - 1], y_ss.at[o - 1], y_rs.at[o - 1],
                   (y2 * NB + b, c)).start()
        else:
            gw[y2] = both

    recv("h")
    h = hz[0].astype(F32)
    for i in range(NZ - 1):
        h = h + hr[i].astype(F32)
    u_own = ub[rows(b, TB), :]
    mixed = dot(mix_ref[...], h * jnp.concatenate([u_own, u_own], axis=1),
                precision=lax.Precision.HIGHEST)
    recv("g")
    g = gz[0].astype(F32)
    for i in range(NZ - 1):
        g = g + gr[i].astype(F32)
    ub[0:128, :] = column(ztot[:, rows(b // 2, 128)])
    z_own = ub[rows(b % 2, SB), :]
    student_f = s_raw / snorm
    student_b = student_f.astype(BF16).astype(F32)
    grad_n = (g / jnp.concatenate([z_own, z_own], axis=1) - mixed) / student_temp
    loss = jnp.log(z_own) - jnp.sum(student_b * mixed, axis=1, keepdims=True) / student_temp
    grad_s = (grad_n - student_f * jnp.sum(student_f * grad_n, axis=1, keepdims=True)) / snorm
    out_ref[c, :, 0:D] = grad_s
    out_ref[c, :, D:] = loss
    out_copy = remote(out_ref.at[c], out_ref.at[c], o_ss, o_rs, (dp, 1 - c))
    out_copy.start()

    grad_w = gw[y]
    for o in range(1, NY):
        recv("y%d" % (o - 1))
        grad_w = grad_w + yr[o - 1].astype(F32)
    grad_w = grad_w / student_temp
    weight_f = proto_f / colnorm
    gv_ref[...] = (
        grad_w - weight_f * jnp.sum(weight_f * grad_w, axis=0, keepdims=True)
    ) / colnorm

    wait_bytes(out_ref.at[1 - c], o_rs)
    out_copy.wait_send()
    finish()


def write_out(out_ref, gv_ref, loss_ref, gs_ref, gw_ref):
    gw_ref[...] = gv_ref[...]
    lane = lax.broadcasted_iota(jnp.int32, (IMG, OUTW - D), 1)
    for half in range(2):
        images = slice(half * IMG, (half + 1) * IMG)
        loss = jnp.zeros((IMG, OUTW - D), F32)
        for crop in range(CROPS):
            rows = slice(crop * IMG, (crop + 1) * IMG)
            gs_ref[crop, images, :] = out_ref[half, rows, 0:D]
            loss = jnp.where(lane == crop, out_ref[half, rows, D:], loss)
        loss_ref[images, :] = loss[:, 0:CROPS]


def shards(teacher_feats, student_feats, proto_v):
    mix = mixing()
    mix_big = jnp.asarray(np.kron(np.eye(8, dtype=np.float32), mix), BF16)
    vmem = pl.BlockSpec(memory_space=pltpu.VMEM)
    dma = pltpu.SemaphoreType.DMA
    out, grad_v = pl.pallas_call(
        kernel,
        out_shape=(
            jax.ShapeDtypeStruct((2, SB, OUTW), F32),
            jax.ShapeDtypeStruct((D, PB), F32),
        ),
        in_specs=[vmem] * 5,
        out_specs=(vmem, vmem),
        scratch_shapes=[
            pltpu.VMEM((NA, D, PB), BF16),
            pltpu.VMEM((TROWS, D), BF16),
            pltpu.VMEM((SROWS, D), BF16),
            pltpu.VMEM((NA, TROWS, PB), F32),
            pltpu.VMEM((NA, TROWS, PB), BF16),
            pltpu.VMEM((NA, SROWS, PB), BF16),
            pltpu.VMEM((D, SROWS), BF16),
            pltpu.VMEM((D, SROWS), BF16),
            pltpu.VMEM((TROWS, 128), F32),
            pltpu.VMEM((NX, ST, D), F32),
            pltpu.VMEM((NX - 1, ST, D), BF16),
            pltpu.VMEM((NX - 1, ST, D), BF16),
            pltpu.VMEM((NZ, SB, D), BF16),
            pltpu.VMEM((NZ - 1, SB, D), BF16),
            pltpu.VMEM((TROWS, D), BF16),
            pltpu.VMEM((NX - 1, NZ * TB, D), BF16),
            pltpu.VMEM((NZ, TB, D), BF16),
            pltpu.VMEM((NZ - 1, TB, D), BF16),
            pltpu.VMEM((NY, D, PB), F32),
            pltpu.VMEM((NY, D, PB), F32),
            pltpu.VMEM((NY, D, PB), F32),
            pltpu.VMEM((NY - 1, D, PB), BF16),
            pltpu.VMEM((NY - 1, D, PB), BF16),
            pltpu.VMEM((SWEEPS, NA, 1, NA * PB), F32),
            pltpu.VMEM((SWEEPS, NB, 1, TROWS), F32),
            pltpu.VMEM((NX - 1, 1, SROWS), F32),
            pltpu.VMEM((NZ - 1, 1, SROWS), F32),
            pltpu.VMEM((1, SROWS), F32),
            pltpu.VMEM((1, SROWS), F32),
            pltpu.VMEM((1, SROWS), F32),
            pltpu.VMEM((TB, D), F32),
            pltpu.VMEM((SB, D), F32),
            pltpu.VMEM((D, TROWS), F32),
            pltpu.VMEM((D, TROWS), F32),
            pltpu.VMEM((NY, TROWS, PB), BF16),
            pltpu.VMEM((2, 1, TROWS), F32),
            dma((2 * NY - 1,)), dma((NA,)),
            dma, dma,
            dma((NZ - 1,)), dma((NZ - 1,)), dma((NX - 1,)), dma((NX - 1,)),
            dma((NX - 1,)), dma((NX - 1,)),
            dma((SWEEPS,)), dma((SWEEPS,)), dma((SWEEPS,)), dma((SWEEPS,)),
            dma, dma, dma, dma, dma, dma,
            dma((NY,)), dma((NY,)),
            dma((NY - 1,)), dma((NY - 1,)),
            dma, dma,
            dma((NY,)), dma((NY,)),
            dma, dma, dma, dma,
            dma, dma, dma, dma,
        ],
        compiler_params=pltpu.CompilerParams(
            collective_id=0, has_side_effects=True, vmem_limit_bytes=56 << 20
        ),
        name="head_step",
    )(teacher_feats, jnp.transpose(student_feats, (1, 0, 2)), proto_v, mix_big, jnp.asarray(mix))
    loss, grad_s, grad_v = pl.pallas_call(
        write_out,
        out_shape=(
            jax.ShapeDtypeStruct((2 * IMG, CROPS), F32),
            jax.ShapeDtypeStruct((CROPS, 2 * IMG, D), F32),
            jax.ShapeDtypeStruct((D, PB), F32),
        ),
        in_specs=[vmem] * 2,
        out_specs=(vmem,) * 3,
        name="write_out",
    )(out, grad_v)
    return (loss, jnp.transpose(grad_s, (1, 0, 2)), grad_v)


def solution(mesh):
    in_specs = (P("dp", None, None), P("dp", None, None), P(None, ("dp", "proto")))
    out_specs = (P("dp", None), P("dp", None, None), P(None, ("dp", "proto")))
    return jax.shard_map(shards, mesh=mesh, in_specs=in_specs, out_specs=out_specs, check_vma=False)
```

```python
import math

import jax
import jax.numpy as jnp
import numpy as np
from jax import lax
from jax.experimental import pallas as pl
from jax.experimental.pallas import tpu as pltpu
from jax.sharding import PartitionSpec as P

MESH = pl.DeviceIdType.MESH
F32, BF16 = jnp.float32, jnp.bfloat16

epsilon = 1e-12
teacher_temp = 0.07
student_temp = 0.1
LOG2E = math.log2(math.e)

NY, NX, NZ = 4, 4, 8
NB, NA = NX * NZ, NY * 2
D = 256
PB = 256
SB, TB = 64, 16
SROWS, TROWS = SB * NB, TB * NB
IMG, CROPS, TEACH = 6, 10, 2
SWEEPS = 3
ST = SB * NZ
OUTW = D + 128


def mixing():
    m = np.zeros((SB, TB), np.float32)
    for img in range(IMG):
        for crop in range(CROPS):
            row, first = crop * IMG + img, img * TEACH
            if crop == 0:
                m[row, first + 1] = 1.0
            elif crop == 1:
                m[row, first] = 1.0
            else:
                m[row, first] = m[row, first + 1] = 0.5
    return m


def dot(x, y, dims=((1,), (0,)), precision=None):
    return lax.dot_general(x, y, (dims, ((), ())), preferred_element_type=F32, precision=precision)


def wait_bytes(ref, sem):
    pltpu.make_async_copy(ref, ref, sem).wait()


def column(row):
    return jnp.broadcast_to(row, (128, 128)).T


def kernel(t_hbm, s_hbm, p_hbm, mix_big_hbm, mix_hbm, out_ref, gv_ref,
           t_ref, s_ref, p_ref, mix_big_ref, mix_ref, in_sem,
           wg, tg, sg, k3, kv, e3, st_ref, szt, ub, gb, gs, gx, gz, gr, hb, hx, hz, hr, gw, cs, cr, ys, yr,
           colbuf, rowbuf, zx, zbuf, zown, ztmp, ztot, traw, sraw, at, ats, kvs, uu,
           w_ss, w_rs, t_ss, t_rs, sz_ss, sz_rs, sx_ss, sx_rs, gx_ss, gx_rs, col_ss, col_rs, row_ss, row_rs, z_ss, z_rs,
           g_ss, g_rs, h_ss, h_rs, c_ss, c_rs, y_ss, y_rs, o_ss, o_rs,
           k_ss, k_rs, at_ss, at_rs, u_ss, u_rs, zx_ss, zx_rs, hx_ss, hx_rs):
    dp = lax.axis_index("dp")
    c = lax.axis_index("proto")
    y, b = dp // NB, dp % NB
    x, zz = b // NZ, b % NZ
    a = y * 2 + c

    def a_dev(a2):
        return ((a2 // 2) * NB + b, a2 % 2)

    def b_dev(b2):
        return (y * NB + b2, c)

    def a_peer(o):
        return (a + o) % NA

    def x_peer(o):
        return (x + o) % NX

    def z_peer(o):
        return (zz + o) % NZ

    def far(i, n):
        return (n // 2 + (2 * (i % 2) - 1) * ((i + 1) // 2)) % n

    def b_far(i):
        return x_peer(far(i % NX, NX)) * NZ + z_peer(far(i // NX, NZ))

    def rows(i, n):
        return pl.ds(pl.multiple_of(i * n, n), n)

    def remote(src, dst, ss, rs, device):
        return pltpu.make_async_remote_copy(
            src_ref=src, dst_ref=dst, send_sem=ss, recv_sem=rs, device_id=device, device_id_type=MESH
        )

    comms = {
        "t": (tg.at[pl.ds(0, (NB - 1) * TB), :], t_ss, t_rs),
        "at": (at, at_ss, at_rs),
        "u": (uu.at[0], u_ss, u_rs),
        "zx": (zx, zx_ss, zx_rs),
        "z": (zbuf, z_ss, z_rs),
        "hx": (hx, hx_ss, hx_rs),
        "g": (gr.at[pl.ds(0, NZ - 1)], g_ss, g_rs),
        "h": (hr, h_ss, h_rs),
    }
    for sweep in range(SWEEPS):
        comms["col%d" % sweep] = (colbuf.at[sweep, pl.ds(0, NA - 1)], col_ss.at[sweep], col_rs.at[sweep])
        comms["row%d" % sweep] = (rowbuf.at[sweep, pl.ds(0, NB - 1)], row_ss.at[sweep], row_rs.at[sweep])
    for z2 in range(1, NZ):
        comms["sz%d" % z2] = (sg.at[pl.ds(0, SB), :], sz_ss.at[z2 - 1], sz_rs.at[z2 - 1])
    for o in range(1, NX):
        comms["sx%d" % o] = (sg.at[pl.ds(0, NZ * SB), :], sx_ss.at[o - 1], sx_rs.at[o - 1])
        comms["gx%d" % o] = (gx.at[o - 1], gx_ss.at[o - 1], gx_rs.at[o - 1])
    for y2 in range(NY):
        comms["c%d" % y2] = (cs.at[y2], c_ss.at[y2], c_rs.at[y2])
        comms["k%d" % y2] = (kvs.at[y2], k_ss.at[y2], k_rs.at[y2])
    for o in range(NY - 1):
        comms["y%d" % o] = (ys.at[o], y_ss.at[o], y_rs.at[o])
    started, received = [], set()

    def recv(name):
        wait_bytes(comms[name][0], comms[name][2])
        received.add(name)

    def finish():
        for name in started:
            if name not in received:
                recv(name)
            wait_bytes(comms[name][0], comms[name][1])
        for cp in w_copies:
            cp.wait_send()

    barrier = pltpu.get_barrier_semaphore()

    @pl.loop(0, NB - 1)
    def _(i):
        pl.semaphore_signal(barrier, inc=1, device_id=b_dev(b_far(i)), device_id_type=MESH)

    @pl.loop(1, NA)
    def _(o):
        pl.semaphore_signal(barrier, inc=1, device_id=a_dev(a_peer(o)), device_id_type=MESH)

    inputs = [
        pltpu.make_async_copy(src, dst, in_sem.at[n])
        for n, (src, dst) in enumerate([
            (p_hbm, p_ref), (t_hbm, t_ref), (s_hbm, s_ref), (mix_big_hbm, mix_big_ref), (mix_hbm, mix_ref)])
    ]
    for cp in inputs:
        cp.start()
    for cp in inputs:
        cp.wait()

    proto_f = p_ref[...].astype(F32)
    colnorm = jnp.sqrt(jnp.sum(proto_f * proto_f, axis=0, keepdims=True) + epsilon)
    wg[a] = (proto_f / colnorm).astype(BF16)
    traw[...] = jnp.zeros_like(traw)
    for img in range(IMG):
        traw[img * TEACH:(img + 1) * TEACH, :] = t_ref[c * IMG + img].astype(F32)
    t_f = traw[...]
    tg[rows(b, TB), :] = (
        t_f / jnp.sqrt(jnp.sum(t_f * t_f, axis=1, keepdims=True) + epsilon)
    ).astype(BF16)
    sraw[...] = jnp.zeros_like(sraw)
    for crop in range(CROPS):
        both = s_ref[crop].astype(F32)
        sraw[crop * IMG:(crop + 1) * IMG, :] = jnp.where(c == 0, both[:IMG], both[IMG:])
    s_raw = sraw[...]
    snorm = jnp.sqrt(jnp.sum(s_raw * s_raw, axis=1, keepdims=True) + epsilon)
    sg[rows(b, SB), :] = (s_raw / snorm).astype(BF16)

    pl.semaphore_wait(barrier, NA - 1 + NB - 1)

    w_copies = []
    for o in (2, 1, 3):
        cp = remote(wg.at[a], wg.at[a], w_ss.at[o - 1], w_rs.at[a], a_dev(a_peer(2 * o)))
        cp.start()
        w_copies.append(cp)

    def b_all(name, src, dst):
        started.append(name)
        _, ss, rs = comms[name]

        @pl.loop(0, NB - 1)
        def _(i):
            b2 = b_far(i)
            remote(src(b2), dst, ss, rs, b_dev(b2)).start()

    def to_sibling(name, src, dst):
        started.append(name)
        remote(src, dst, comms[name][1], comms[name][2], (dp, 1 - c)).start()

    t_own = tg.at[rows(b, TB), :]
    b_all("t", lambda _: t_own, t_own)
    cp = remote(wg.at[a], wg.at[a], w_ss.at[NY - 1], w_rs.at[a], (dp, 1 - c))
    cp.start()
    w_copies.append(cp)
    s_own = sg.at[rows(b, SB), :]

    def s_forward(z2):
        src = sg.at[rows(x * NZ + z2, SB), :]
        for o in range(1, NX):
            remote(src, src, sx_ss.at[o - 1], sx_rs.at[o - 1], b_dev(x_peer(o) * NZ + zz)).start()

    z_order = [1, 7, 2, 6, 3, 5, 4]
    for o in z_order:
        started.append("sz%d" % o)
        remote(s_own, s_own, sz_ss.at[o - 1], sz_rs.at[o - 1], b_dev(x * NZ + z_peer(o))).start()
    for o in range(1, NX):
        started.append("sx%d" % o)
    s_forward(zz)

    for o in range(1, NY):
        a2 = a_peer(2 * (NY - o))
        wait_bytes(wg.at[a2], w_rs.at[a2])
        cp = remote(wg.at[a2], wg.at[a2], w_ss.at[NY - 1 + o], w_rs.at[a2], (dp, 1 - c))
        cp.start()
        w_copies.append(cp)
    def s_on(offsets):
        for o in offsets:
            recv("sz%d" % o)
            s_forward(z_peer(NZ - o))

    s_on((7, 1, 6, 2))
    recv("t")
    valid = (lax.broadcasted_iota(jnp.int32, (1, TROWS), 1) % TB < IMG * TEACH).astype(F32)

    def set_u(u_row):
        for r in range(TROWS // 128):
            ub[r * 128:(r + 1) * 128, :] = column(u_row[:, r * 128:(r + 1) * 128])

    set_u(valid)

    def col_send(sweep):
        src = colbuf.at[sweep, a]
        started.append("col%d" % sweep)

        @pl.loop(1, NA)
        def _(o):
            remote(src, src, col_ss.at[sweep], col_rs.at[sweep], a_dev(a_peer(o))).start()

    def col_wait(sweep):
        recv("col%d" % sweep)
        total = colbuf[sweep, 0]
        for i in range(1, NA):
            total = total + colbuf[sweep, i]
        return 1.0 / total

    def row_send(sweep):
        src = rowbuf.at[sweep, b]
        b_all("row%d" % sweep, lambda _: src, src)

    def row_wait(sweep):
        recv("row%d" % sweep)
        total = rowbuf[sweep, 0]
        for i in range(1, NB):
            total = total + rowbuf[sweep, i]
        return valid / total

    def col_part(sweep):
        @pl.loop(0, NA)
        def _(i):
            u2 = ub[...]
            part = jnp.sum(k3[i] * jnp.concatenate([u2, u2], axis=1), axis=0, keepdims=True)
            colbuf[sweep, a, :, rows(i, PB)] = part

    def row_part(sweep, v, last):
        @pl.loop(0, TROWS // 128)
        def _(r):
            acc = jnp.zeros((128, 128), F32)
            h = jnp.zeros((128, D), F32)
            for i in range(NA):
                scaled = k3[i, rows(r, 128), :] * v[:, i * PB:(i + 1) * PB]
                acc = acc + scaled[:, :128] + scaled[:, 128:]
                if last:
                    scaled = scaled.astype(BF16)
                    kv[i, rows(r, 128), :] = scaled
                    h = h + dot(scaled, wg[i], ((1,), (1,)))
            rowbuf[sweep, b, :, rows(r, 128)] = jnp.sum(acc.T, axis=0, keepdims=True)
            if last:
                hb[rows(r, 128), :] = h.astype(BF16)

    def targets(i):
        k = jnp.exp2(dot(tg[...], wg[i]) * (LOG2E / teacher_temp))
        k3[i] = k
        u2 = ub[...]
        colbuf[0, a, :, rows(i, PB)] = jnp.sum(
            k * jnp.concatenate([u2, u2], axis=1), axis=0, keepdims=True)

    def student(step):
        @pl.loop(step, step + 1)
        def _(step):
            r = x_peer(NX - step)
            feats = sg[rows(r, ST), :]
            z = jnp.zeros((ST, 128), F32)
            g = jnp.zeros((ST, D), F32)
            for i in range(NA):
                e = jnp.exp2(dot(feats, wg[i]) * (LOG2E / student_temp))
                z = z + e[:, :128] + e[:, 128:]
                e = e.astype(BF16)
                e3[i, rows(r, ST), :] = e
                g = g + dot(e, wg[i], ((1,), (1,)))
            gb[step] = g
            for j in range(ST // 128):
                part = jnp.sum(z[j * 128:(j + 1) * 128, :].T, axis=0, keepdims=True)
                zown[:, pl.ds(pl.multiple_of(r * ST, ST) + j * 128, 128)] = part
                f_t = feats[j * 128:(j + 1) * 128, :].astype(F32).T
                st_ref[:, pl.ds(pl.multiple_of(r * ST, ST) + j * 128, 128)] = f_t.astype(BF16)

    def student_send(step):
        if step:
            o = NX - step
            gs[step - 1] = gb[step].astype(BF16)
            started.append("gx%d" % o)
            remote(gs.at[step - 1], gx.at[o - 1], gx_ss.at[o - 1], gx_rs.at[o - 1],
                   b_dev(x_peer(o) * NZ + zz)).start()

    def student_step(step):
        if step:
            recv("sx%d" % step)
        student(step)

    targets(a)
    for o in range(1, NY):
        targets(a_peer(2 * (NY - o)))
    for o in (0, 3, 2, 1):
        a2 = ((y + o) % NY) * 2 + 1 - c
        wait_bytes(wg.at[a2], w_rs.at[a2])
        targets(a2)
    col_send(0)
    s_on((5, 3, 4))
    student_step(0)
    v = col_wait(0)
    row_part(0, v, False)
    row_send(0)
    student_step(1)
    student_step(3)
    set_u(row_wait(0))
    col_part(1)
    col_send(1)
    student_send(1)
    student_send(3)
    student_step(2)
    started.append("zx")
    for o in range(1, NX):
        remote(zown, zx.at[o - 1], zx_ss, zx_rs, b_dev(x_peer(o) * NZ + zz)).start()
    v = col_wait(1)
    row_part(1, v, False)
    row_send(1)
    recv("zx")
    ztmp[...] = zown[...] + zx[0] + zx[1] + zx[2]
    set_u(row_wait(1))
    col_part(2)
    col_send(2)
    student_send(2)
    started.append("z")
    for o in z_order:
        remote(ztmp, zbuf.at[o - 1], z_ss, z_rs, b_dev(x * NZ + z_peer(o))).start()
    for j in range(TROWS // 128):
        at[:, j * 128:(j + 1) * 128] = dot(st_ref[:, j * 512:(j + 1) * 512], mix_big_ref[...])
    to_sibling("at", at, ats)
    v = col_wait(2)
    row_part(2, v, True)
    row_send(2)
    started.append("hx")
    for o in range(1, NX):
        remote(hb.at[rows(x_peer(o), NZ * TB), :], hx.at[o - 1], hx_ss, hx_rs,
               b_dev(x_peer(o) * NZ + zz)).start()
    for y2 in range(NY):
        to_sibling("k%d" % y2, kv.at[y2 * 2 + 1 - c], kvs.at[y2])
    recv("z")
    zsum = ztmp[...]
    for i in range(NZ - 1):
        zsum = zsum + zbuf[i]
    ztot[...] = zsum
    z_inv = 1.0 / zsum
    for j in range(SROWS // 512):
        szt[:, j * 512:(j + 1) * 512] = (
            st_ref[:, j * 512:(j + 1) * 512].astype(F32) * z_inv[:, j * 512:(j + 1) * 512]
        ).astype(BF16)
    for y2 in range(NY):
        cs[y2] = dot(szt[...], e3[y2 * 2 + 1 - c])
        to_sibling("c%d" % y2, cs.at[y2], cr.at[y2])
    for y2 in range(NY):
        gw[y2] = dot(szt[...], e3[y2 * 2 + c])
    for o in range(1, NX):
        recv("gx%d" % o)
    started.append("g")
    for o in z_order + [0]:
        z2 = z_peer(o)
        g = gb[0, rows(z2, SB), :]
        for i in range(NX - 1):
            g = g + gx[i, rows(z2, SB), :].astype(F32)
        gz[o] = g.astype(BF16)
        if o:
            remote(gz.at[o], gr.at[o - 1], g_ss, g_rs, b_dev(x * NZ + z2)).start()
    recv("hx")
    started.append("h")
    for o in z_order + [0]:
        z2 = z_peer(o)
        h = hb[rows(x * NZ + z2, TB), :].astype(F32)
        for i in range(NX - 1):
            h = h + hx[i, rows(z2, TB), :].astype(F32)
        hz[o] = h.astype(BF16)
        if o:
            remote(hz.at[o], hr.at[o - 1], h_ss, h_rs, b_dev(x * NZ + z2)).start()
    u_row = row_wait(2)
    uu[c] = u_row
    to_sibling("u", uu.at[c], uu.at[c])
    set_u(u_row)

    def scaled_mix(mixed_t, u2):
        full = mixed_t * u2
        high = full.astype(BF16)
        return jnp.concatenate([high, (full - high.astype(F32)).astype(BF16)], axis=0)

    def teacher_part(ua, k2):
        both = dot(ua, k2)
        return both[:D] + both[D:]

    ua = scaled_mix(at[...], u_row)
    for y2 in range(NY):
        gw[y2] = gw[y2] - teacher_part(ua, kv[y2 * 2 + c])
    recv("at")
    recv("u")
    ua = scaled_mix(ats[...], uu[1 - c])
    for name in range(NY):
        recv("k%d" % name)
        recv("c%d" % name)
    for o in (2, 1, 3, 0):
        y2 = (y + o) % NY
        both = gw[y2] + cr[y2] - teacher_part(ua, kvs[y2])
        if o:
            ys[o - 1] = both.astype(BF16)
            started.append("y%d" % (o - 1))
            remote(ys.at[o - 1], yr.at[o - 1], y_ss.at[o - 1], y_rs.at[o - 1],
                   (y2 * NB + b, c)).start()
        else:
            gw[y2] = both

    recv("h")
    h = hz[0].astype(F32)
    for i in range(NZ - 1):
        h = h + hr[i].astype(F32)
    u_own = ub[rows(b, TB), :]
    mixed = dot(mix_ref[...], h * jnp.concatenate([u_own, u_own], axis=1),
                precision=lax.Precision.HIGHEST)
    recv("g")
    g = gz[0].astype(F32)
    for i in range(NZ - 1):
        g = g + gr[i].astype(F32)
    ub[0:128, :] = column(ztot[:, rows(b // 2, 128)])
    z_own = ub[rows(b % 2, SB), :]
    student_f = s_raw / snorm
    student_b = student_f.astype(BF16).astype(F32)
    grad_n = (g / jnp.concatenate([z_own, z_own], axis=1) - mixed) / student_temp
    loss = jnp.log(z_own) - jnp.sum(student_b * mixed, axis=1, keepdims=True) / student_temp
    grad_s = (grad_n - student_f * jnp.sum(student_f * grad_n, axis=1, keepdims=True)) / snorm
    out_ref[c, :, 0:D] = grad_s
    out_ref[c, :, D:] = loss
    out_copy = remote(out_ref.at[c], out_ref.at[c], o_ss, o_rs, (dp, 1 - c))
    out_copy.start()

    grad_w = gw[y]
    for o in range(1, NY):
        recv("y%d" % (o - 1))
        grad_w = grad_w + yr[o - 1].astype(F32)
    grad_w = grad_w / student_temp
    weight_f = proto_f / colnorm
    gv_ref[...] = (
        grad_w - weight_f * jnp.sum(weight_f * grad_w, axis=0, keepdims=True)
    ) / colnorm

    wait_bytes(out_ref.at[1 - c], o_rs)
    out_copy.wait_send()
    finish()


def write_out(out_ref, gv_ref, loss_ref, gs_ref, gw_ref):
    gw_ref[...] = gv_ref[...]
    lane = lax.broadcasted_iota(jnp.int32, (IMG, OUTW - D), 1)
    for half in range(2):
        images = slice(half * IMG, (half + 1) * IMG)
        loss = jnp.zeros((IMG, OUTW - D), F32)
        for crop in range(CROPS):
            rows = slice(crop * IMG, (crop + 1) * IMG)
            gs_ref[crop, images, :] = out_ref[half, rows, 0:D]
            loss = jnp.where(lane == crop, out_ref[half, rows, D:], loss)
        loss_ref[images, :] = loss[:, 0:CROPS]


def shards(teacher_feats, student_feats, proto_v):
    mix = mixing()
    mix_big = jnp.asarray(np.kron(np.eye(8, dtype=np.float32), mix), BF16)
    vmem = pl.BlockSpec(memory_space=pltpu.VMEM)
    dma = pltpu.SemaphoreType.DMA
    out, grad_v = pl.pallas_call(
        kernel,
        out_shape=(
            jax.ShapeDtypeStruct((2, SB, OUTW), F32),
            jax.ShapeDtypeStruct((D, PB), F32),
        ),
        in_specs=[pl.BlockSpec(memory_space=pl.ANY)] * 5,
        out_specs=(vmem, vmem),
        scratch_shapes=[
            pltpu.VMEM((2 * IMG, TEACH, D), BF16),
            pltpu.VMEM((CROPS, 2 * IMG, D), BF16),
            pltpu.VMEM((D, PB), BF16),
            pltpu.VMEM((8 * SB, 8 * TB), BF16),
            pltpu.VMEM((SB, TB), F32),
            dma((5,)),
            pltpu.VMEM((NA, D, PB), BF16),
            pltpu.VMEM((TROWS, D), BF16),
            pltpu.VMEM((SROWS, D), BF16),
            pltpu.VMEM((NA, TROWS, PB), F32),
            pltpu.VMEM((NA, TROWS, PB), BF16),
            pltpu.VMEM((NA, SROWS, PB), BF16),
            pltpu.VMEM((D, SROWS), BF16),
            pltpu.VMEM((D, SROWS), BF16),
            pltpu.VMEM((TROWS, 128), F32),
            pltpu.VMEM((NX, ST, D), F32),
            pltpu.VMEM((NX - 1, ST, D), BF16),
            pltpu.VMEM((NX - 1, ST, D), BF16),
            pltpu.VMEM((NZ, SB, D), BF16),
            pltpu.VMEM((NZ - 1, SB, D), BF16),
            pltpu.VMEM((TROWS, D), BF16),
            pltpu.VMEM((NX - 1, NZ * TB, D), BF16),
            pltpu.VMEM((NZ, TB, D), BF16),
            pltpu.VMEM((NZ - 1, TB, D), BF16),
            pltpu.VMEM((NY, D, PB), F32),
            pltpu.VMEM((NY, D, PB), F32),
            pltpu.VMEM((NY, D, PB), F32),
            pltpu.VMEM((NY - 1, D, PB), BF16),
            pltpu.VMEM((NY - 1, D, PB), BF16),
            pltpu.VMEM((SWEEPS, NA, 1, NA * PB), F32),
            pltpu.VMEM((SWEEPS, NB, 1, TROWS), F32),
            pltpu.VMEM((NX - 1, 1, SROWS), F32),
            pltpu.VMEM((NZ - 1, 1, SROWS), F32),
            pltpu.VMEM((1, SROWS), F32),
            pltpu.VMEM((1, SROWS), F32),
            pltpu.VMEM((1, SROWS), F32),
            pltpu.VMEM((TB, D), F32),
            pltpu.VMEM((SB, D), F32),
            pltpu.VMEM((D, TROWS), F32),
            pltpu.VMEM((D, TROWS), F32),
            pltpu.VMEM((NY, TROWS, PB), BF16),
            pltpu.VMEM((2, 1, TROWS), F32),
            dma((2 * NY - 1,)), dma((NA,)),
            dma, dma,
            dma((NZ - 1,)), dma((NZ - 1,)), dma((NX - 1,)), dma((NX - 1,)),
            dma((NX - 1,)), dma((NX - 1,)),
            dma((SWEEPS,)), dma((SWEEPS,)), dma((SWEEPS,)), dma((SWEEPS,)),
            dma, dma, dma, dma, dma, dma,
            dma((NY,)), dma((NY,)),
            dma((NY - 1,)), dma((NY - 1,)),
            dma, dma,
            dma((NY,)), dma((NY,)),
            dma, dma, dma, dma,
            dma, dma, dma, dma,
        ],
        compiler_params=pltpu.CompilerParams(
            collective_id=0, has_side_effects=True, vmem_limit_bytes=56 << 20
        ),
        name="head_step",
    )(teacher_feats, jnp.transpose(student_feats, (1, 0, 2)), proto_v, mix_big, jnp.asarray(mix))
    loss, grad_s, grad_v = pl.pallas_call(
        write_out,
        out_shape=(
            jax.ShapeDtypeStruct((2 * IMG, CROPS), F32),
            jax.ShapeDtypeStruct((CROPS, 2 * IMG, D), F32),
            jax.ShapeDtypeStruct((D, PB), F32),
        ),
        in_specs=[vmem] * 2,
        out_specs=(vmem,) * 3,
        name="write_out",
    )(out, grad_v)
    return (loss, jnp.transpose(grad_s, (1, 0, 2)), grad_v)


def solution(mesh):
    in_specs = (P("dp", None, None), P("dp", None, None), P(None, ("dp", "proto")))
    out_specs = (P("dp", None), P("dp", None, None), P(None, ("dp", "proto")))
    return jax.shard_map(shards, mesh=mesh, in_specs=in_specs, out_specs=out_specs, check_vma=False)
```

```python
import math

import jax
import jax.numpy as jnp
import numpy as np
from jax import lax
from jax.experimental import pallas as pl
from jax.experimental.pallas import tpu as pltpu
from jax.sharding import PartitionSpec as P

MESH = pl.DeviceIdType.MESH
F32, BF16 = jnp.float32, jnp.bfloat16

epsilon = 1e-12
teacher_temp = 0.07
student_temp = 0.1
LOG2E = math.log2(math.e)

NY, NX, NZ = 4, 4, 8
NB, NA = NX * NZ, NY * 2
D = 256
PB = 256
SB, TB = 64, 16
SROWS, TROWS = SB * NB, TB * NB
IMG, CROPS, TEACH = 6, 10, 2
SWEEPS = 3
ST = SB * NZ
OUTW = D + 128


def mixing():
    m = np.zeros((SB, TB), np.float32)
    for img in range(IMG):
        for crop in range(CROPS):
            row, first = crop * IMG + img, img * TEACH
            if crop == 0:
                m[row, first + 1] = 1.0
            elif crop == 1:
                m[row, first] = 1.0
            else:
                m[row, first] = m[row, first + 1] = 0.5
    return m


def dot(x, y, dims=((1,), (0,)), precision=None):
    return lax.dot_general(x, y, (dims, ((), ())), preferred_element_type=F32, precision=precision)


def wait_bytes(ref, sem):
    pltpu.make_async_copy(ref, ref, sem).wait()


def column(row):
    return jnp.broadcast_to(row, (128, 128)).T


def kernel(t_hbm, s_hbm, p_hbm, mix_big_hbm, mix_hbm, out_ref, gv_ref,
           t_ref, s_ref, p_ref, mix_big_ref, mix_ref, in_sem,
           wg, tg, sg, k3, kv, e3, st_ref, szt, ub, gb, gs, gx, gz, gr, hb, hx, hz, hr, gw, cs, cr, ys, yr,
           colbuf, rowbuf, zx, zbuf, zown, ztmp, ztot, traw, sraw, at, ats, kvs, uu,
           w_ss, w_rs, tz_ss, tz_rs, tx_ss, tx_rs, sz_ss, sz_rs, sx_ss, sx_rs, gx_ss, gx_rs, col_ss, col_rs, row_ss, row_rs, z_ss, z_rs,
           g_ss, g_rs, h_ss, h_rs, c_ss, c_rs, y_ss, y_rs, o_ss, o_rs,
           k_ss, k_rs, at_ss, at_rs, u_ss, u_rs, zx_ss, zx_rs, hx_ss, hx_rs):
    dp = lax.axis_index("dp")
    c = lax.axis_index("proto")
    y, b = dp // NB, dp % NB
    x, zz = b // NZ, b % NZ
    a = y * 2 + c

    def a_dev(a2):
        return ((a2 // 2) * NB + b, a2 % 2)

    def b_dev(b2):
        return (y * NB + b2, c)

    def a_peer(o):
        return (a + o) % NA

    def x_peer(o):
        return (x + o) % NX

    def z_peer(o):
        return (zz + o) % NZ

    def far(i, n):
        return (n // 2 + (2 * (i % 2) - 1) * ((i + 1) // 2)) % n

    def b_far(i):
        return x_peer(far(i % NX, NX)) * NZ + z_peer(far(i // NX, NZ))

    def rows(i, n):
        return pl.ds(pl.multiple_of(i * n, n), n)

    def remote(src, dst, ss, rs, device):
        return pltpu.make_async_remote_copy(
            src_ref=src, dst_ref=dst, send_sem=ss, recv_sem=rs, device_id=device, device_id_type=MESH
        )

    comms = {
        "at": (at, at_ss, at_rs),
        "u": (uu.at[0], u_ss, u_rs),
        "zx": (zx, zx_ss, zx_rs),
        "z": (zbuf, z_ss, z_rs),
        "hx": (hx, hx_ss, hx_rs),
        "g": (gr.at[pl.ds(0, NZ - 1)], g_ss, g_rs),
        "h": (hr, h_ss, h_rs),
    }
    for sweep in range(SWEEPS):
        comms["col%d" % sweep] = (colbuf.at[sweep, pl.ds(0, NA - 1)], col_ss.at[sweep], col_rs.at[sweep])
        comms["row%d" % sweep] = (rowbuf.at[sweep, pl.ds(0, NB - 1)], row_ss.at[sweep], row_rs.at[sweep])
    for z2 in range(1, NZ):
        comms["tz%d" % z2] = (tg.at[pl.ds(0, TB), :], tz_ss.at[z2 - 1], tz_rs.at[z2 - 1])
        comms["sz%d" % z2] = (sg.at[pl.ds(0, SB), :], sz_ss.at[z2 - 1], sz_rs.at[z2 - 1])
    for o in range(1, NX):
        comms["tx%d" % o] = (tg.at[pl.ds(0, NZ * TB), :], tx_ss.at[o - 1], tx_rs.at[o - 1])
        comms["sx%d" % o] = (sg.at[pl.ds(0, NZ * SB), :], sx_ss.at[o - 1], sx_rs.at[o - 1])
        comms["gx%d" % o] = (gx.at[o - 1], gx_ss.at[o - 1], gx_rs.at[o - 1])
    for y2 in range(NY):
        comms["c%d" % y2] = (cs.at[y2], c_ss.at[y2], c_rs.at[y2])
        comms["k%d" % y2] = (kvs.at[y2], k_ss.at[y2], k_rs.at[y2])
    for o in range(NY - 1):
        comms["y%d" % o] = (ys.at[o], y_ss.at[o], y_rs.at[o])
    started, received = [], set()

    def recv(name):
        wait_bytes(comms[name][0], comms[name][2])
        received.add(name)

    def finish():
        for name in started:
            if name not in received:
                recv(name)
            wait_bytes(comms[name][0], comms[name][1])
        for cp in w_copies:
            cp.wait_send()

    barrier = pltpu.get_barrier_semaphore()

    @pl.loop(0, NB - 1)
    def _(i):
        pl.semaphore_signal(barrier, inc=1, device_id=b_dev(b_far(i)), device_id_type=MESH)

    @pl.loop(1, NA)
    def _(o):
        pl.semaphore_signal(barrier, inc=1, device_id=a_dev(a_peer(o)), device_id_type=MESH)

    inputs = [
        pltpu.make_async_copy(src, dst, in_sem.at[n])
        for n, (src, dst) in enumerate([
            (p_hbm, p_ref), (t_hbm, t_ref), (s_hbm, s_ref), (mix_big_hbm, mix_big_ref), (mix_hbm, mix_ref)])
    ]
    for cp in inputs:
        cp.start()
    for cp in inputs:
        cp.wait()

    proto_f = p_ref[...].astype(F32)
    colnorm = jnp.sqrt(jnp.sum(proto_f * proto_f, axis=0, keepdims=True) + epsilon)
    wg[a] = (proto_f / colnorm).astype(BF16)
    traw[...] = jnp.zeros_like(traw)
    for img in range(IMG):
        traw[img * TEACH:(img + 1) * TEACH, :] = t_ref[c * IMG + img].astype(F32)
    t_f = traw[...]
    tg[rows(b, TB), :] = (
        t_f / jnp.sqrt(jnp.sum(t_f * t_f, axis=1, keepdims=True) + epsilon)
    ).astype(BF16)
    sraw[...] = jnp.zeros_like(sraw)
    for crop in range(CROPS):
        both = s_ref[crop].astype(F32)
        sraw[crop * IMG:(crop + 1) * IMG, :] = jnp.where(c == 0, both[:IMG], both[IMG:])
    s_raw = sraw[...]
    snorm = jnp.sqrt(jnp.sum(s_raw * s_raw, axis=1, keepdims=True) + epsilon)
    sg[rows(b, SB), :] = (s_raw / snorm).astype(BF16)

    pl.semaphore_wait(barrier, NA - 1 + NB - 1)

    w_copies = []
    for o in (1, 3, 2):
        cp = remote(wg.at[a], wg.at[a], w_ss.at[o - 1], w_rs.at[a], a_dev(a_peer(2 * o)))
        cp.start()
        w_copies.append(cp)

    def b_all(name, src, dst):
        started.append(name)
        _, ss, rs = comms[name]

        @pl.loop(0, NB - 1)
        def _(i):
            b2 = b_far(i)
            remote(src(b2), dst, ss, rs, b_dev(b2)).start()

    def to_sibling(name, src, dst):
        started.append(name)
        remote(src, dst, comms[name][1], comms[name][2], (dp, 1 - c)).start()

    t_own = tg.at[rows(b, TB), :]
    def t_forward(z2):
        src = tg.at[rows(x * NZ + z2, TB), :]
        for o in (2, 1, 3):
            remote(src, src, tx_ss.at[o - 1], tx_rs.at[o - 1], b_dev(x_peer(o) * NZ + zz)).start()

    for o in (4, 3, 5, 2, 6, 1, 7):
        started.append("tz%d" % o)
        remote(t_own, t_own, tz_ss.at[o - 1], tz_rs.at[o - 1], b_dev(x * NZ + z_peer(o))).start()
    for o in range(1, NX):
        started.append("tx%d" % o)
    t_forward(zz)
    cp = remote(wg.at[a], wg.at[a], w_ss.at[NY - 1], w_rs.at[a], (dp, 1 - c))
    cp.start()
    w_copies.append(cp)
    s_own = sg.at[rows(b, SB), :]

    def s_forward(z2):
        src = sg.at[rows(x * NZ + z2, SB), :]
        for o in range(1, NX):
            remote(src, src, sx_ss.at[o - 1], sx_rs.at[o - 1], b_dev(x_peer(o) * NZ + zz)).start()

    z_order = [1, 7, 2, 6, 3, 5, 4]
    for o in z_order:
        started.append("sz%d" % o)
        remote(s_own, s_own, sz_ss.at[o - 1], sz_rs.at[o - 1], b_dev(x * NZ + z_peer(o))).start()
    for o in range(1, NX):
        started.append("sx%d" % o)
    s_forward(zz)

    for o in (7, 1, 6, 2, 5, 3, 4):
        recv("tz%d" % o)
        t_forward(z_peer(NZ - o))
    for o in (1, 3, 2):
        a2 = a_peer(2 * (NY - o))
        wait_bytes(wg.at[a2], w_rs.at[a2])
        cp = remote(wg.at[a2], wg.at[a2], w_ss.at[NY - 1 + o], w_rs.at[a2], (dp, 1 - c))
        cp.start()
        w_copies.append(cp)
    def s_on(offsets):
        for o in offsets:
            recv("sz%d" % o)
            s_forward(z_peer(NZ - o))

    s_on((7, 1, 6, 2))
    for o in range(1, NX):
        recv("tx%d" % o)
    valid = (lax.broadcasted_iota(jnp.int32, (1, TROWS), 1) % TB < IMG * TEACH).astype(F32)

    def set_u(u_row):
        for r in range(TROWS // 128):
            ub[r * 128:(r + 1) * 128, :] = column(u_row[:, r * 128:(r + 1) * 128])

    set_u(valid)

    def col_send(sweep):
        src = colbuf.at[sweep, a]
        started.append("col%d" % sweep)

        @pl.loop(1, NA)
        def _(o):
            remote(src, src, col_ss.at[sweep], col_rs.at[sweep], a_dev(a_peer(o))).start()

    def col_wait(sweep):
        recv("col%d" % sweep)
        total = colbuf[sweep, 0]
        for i in range(1, NA):
            total = total + colbuf[sweep, i]
        return 1.0 / total

    def row_send(sweep):
        src = rowbuf.at[sweep, b]
        b_all("row%d" % sweep, lambda _: src, src)

    def row_wait(sweep):
        recv("row%d" % sweep)
        total = rowbuf[sweep, 0]
        for i in range(1, NB):
            total = total + rowbuf[sweep, i]
        return valid / total

    def col_part(sweep):
        @pl.loop(0, NA)
        def _(i):
            u2 = ub[...]
            part = jnp.sum(k3[i] * jnp.concatenate([u2, u2], axis=1), axis=0, keepdims=True)
            colbuf[sweep, a, :, rows(i, PB)] = part

    def row_part(sweep, v):
        @pl.loop(0, TROWS // 128)
        def _(r):
            acc = jnp.zeros((128, 128), F32)
            for i in range(NA):
                scaled = k3[i, rows(r, 128), :] * v[:, i * PB:(i + 1) * PB]
                acc = acc + scaled[:, :128] + scaled[:, 128:]
            rowbuf[sweep, b, :, rows(r, 128)] = jnp.sum(acc.T, axis=0, keepdims=True)

    def teacher_grad(v):
        @pl.loop(0, TROWS // 256)
        def _(r):
            h = jnp.zeros((256, D), F32)
            for i in range(NA):
                scaled = (k3[i, rows(r, 256), :] * v[:, i * PB:(i + 1) * PB]).astype(BF16)
                kv[i, rows(r, 256), :] = scaled
                h = h + dot(scaled, wg[i], ((1,), (1,)))
            hb[rows(r, 256), :] = h.astype(BF16)

    def targets(i):
        k = jnp.exp2(dot(tg[...], wg[i]) * (LOG2E / teacher_temp))
        k3[i] = k
        u2 = ub[...]
        colbuf[0, a, :, rows(i, PB)] = jnp.sum(
            k * jnp.concatenate([u2, u2], axis=1), axis=0, keepdims=True)

    def student(step):
        @pl.loop(step, step + 1)
        def _(step):
            r = x_peer(NX - step)
            feats = sg[rows(r, ST), :]
            z = jnp.zeros((ST, 128), F32)
            g = jnp.zeros((ST, D), F32)
            for i in range(NA):
                e = jnp.exp2(dot(feats, wg[i]) * (LOG2E / student_temp))
                z = z + e[:, :128] + e[:, 128:]
                e = e.astype(BF16)
                e3[i, rows(r, ST), :] = e
                g = g + dot(e, wg[i], ((1,), (1,)))
            gb[step] = g
            for j in range(ST // 128):
                part = jnp.sum(z[j * 128:(j + 1) * 128, :].T, axis=0, keepdims=True)
                zown[:, pl.ds(pl.multiple_of(r * ST, ST) + j * 128, 128)] = part
                f_t = feats[j * 128:(j + 1) * 128, :].astype(F32).T
                st_ref[:, pl.ds(pl.multiple_of(r * ST, ST) + j * 128, 128)] = f_t.astype(BF16)

    def student_send(step):
        if step:
            o = NX - step
            gs[step - 1] = gb[step].astype(BF16)
            started.append("gx%d" % o)
            remote(gs.at[step - 1], gx.at[o - 1], gx_ss.at[o - 1], gx_rs.at[o - 1],
                   b_dev(x_peer(o) * NZ + zz)).start()

    def student_step(step):
        if step:
            recv("sx%d" % step)
        student(step)

    targets(a)
    for o in range(1, NY):
        targets(a_peer(2 * (NY - o)))
    for o in (0, 3, 1, 2):
        a2 = ((y + o) % NY) * 2 + 1 - c
        wait_bytes(wg.at[a2], w_rs.at[a2])
        targets(a2)
    col_send(0)
    s_on((5, 3, 4))
    student_step(0)
    v = col_wait(0)
    row_part(0, v)
    row_send(0)
    student_step(1)
    student_step(3)
    set_u(row_wait(0))
    col_part(1)
    col_send(1)
    student_send(1)
    student_send(3)
    student_step(2)
    started.append("zx")
    for o in range(1, NX):
        remote(zown, zx.at[o - 1], zx_ss, zx_rs, b_dev(x_peer(o) * NZ + zz)).start()
    v = col_wait(1)
    row_part(1, v)
    row_send(1)
    recv("zx")
    ztmp[...] = zown[...] + zx[0] + zx[1] + zx[2]
    started.append("z")
    for o in z_order:
        remote(ztmp, zbuf.at[o - 1], z_ss, z_rs, b_dev(x * NZ + z_peer(o))).start()
    set_u(row_wait(1))
    col_part(2)
    col_send(2)
    student_send(2)
    for j in range(TROWS // 128):
        at[:, j * 128:(j + 1) * 128] = dot(st_ref[:, j * 512:(j + 1) * 512], mix_big_ref[...])
    to_sibling("at", at, ats)
    recv("z")
    zsum = ztmp[...]
    for i in range(NZ - 1):
        zsum = zsum + zbuf[i]
    ztot[...] = zsum
    z_inv = 1.0 / zsum
    for j in range(SROWS // 512):
        szt[:, j * 512:(j + 1) * 512] = (
            st_ref[:, j * 512:(j + 1) * 512].astype(F32) * z_inv[:, j * 512:(j + 1) * 512]
        ).astype(BF16)
    for y2 in range(NY):
        cs[y2] = dot(szt[...], e3[y2 * 2 + 1 - c])
        to_sibling("c%d" % y2, cs.at[y2], cr.at[y2])
    for y2 in range(NY):
        gw[y2] = dot(szt[...], e3[y2 * 2 + c])
    v = col_wait(2)
    row_part(2, v)
    row_send(2)
    teacher_grad(v)
    started.append("hx")
    for o in range(1, NX):
        remote(hb.at[rows(x_peer(o), NZ * TB), :], hx.at[o - 1], hx_ss, hx_rs,
               b_dev(x_peer(o) * NZ + zz)).start()
    for y2 in range(NY):
        to_sibling("k%d" % y2, kv.at[y2 * 2 + 1 - c], kvs.at[y2])
    for o in range(1, NX):
        recv("gx%d" % o)
    started.append("g")
    for o in z_order + [0]:
        z2 = z_peer(o)
        g = gb[0, rows(z2, SB), :]
        for i in range(NX - 1):
            g = g + gx[i, rows(z2, SB), :].astype(F32)
        gz[o] = g.astype(BF16)
        if o:
            remote(gz.at[o], gr.at[o - 1], g_ss, g_rs, b_dev(x * NZ + z2)).start()
    u_row = row_wait(2)
    uu[c] = u_row
    to_sibling("u", uu.at[c], uu.at[c])
    set_u(u_row)

    def scaled_mix(mixed_t, u2):
        full = mixed_t * u2
        high = full.astype(BF16)
        return jnp.concatenate([high, (full - high.astype(F32)).astype(BF16)], axis=0)

    def teacher_part(ua, k2):
        both = dot(ua, k2)
        return both[:D] + both[D:]

    ua = scaled_mix(at[...], u_row)
    for y2 in range(NY):
        gw[y2] = gw[y2] - teacher_part(ua, kv[y2 * 2 + c])
    recv("hx")
    started.append("h")
    for o in z_order + [0]:
        z2 = z_peer(o)
        h = hb[rows(x * NZ + z2, TB), :].astype(F32)
        for i in range(NX - 1):
            h = h + hx[i, rows(z2, TB), :].astype(F32)
        hz[o] = h.astype(BF16)
        if o:
            remote(hz.at[o], hr.at[o - 1], h_ss, h_rs, b_dev(x * NZ + z2)).start()
    recv("at")
    recv("u")
    ua = scaled_mix(ats[...], uu[1 - c])
    for name in range(NY):
        recv("k%d" % name)
        recv("c%d" % name)
    for o in (2, 1, 3, 0):
        y2 = (y + o) % NY
        both = gw[y2] + cr[y2] - teacher_part(ua, kvs[y2])
        if o:
            ys[o - 1] = both.astype(BF16)
            started.append("y%d" % (o - 1))
            remote(ys.at[o - 1], yr.at[o - 1], y_ss.at[o - 1], y_rs.at[o - 1],
                   (y2 * NB + b, c)).start()
        else:
            gw[y2] = both

    recv("h")
    h = hz[0].astype(F32)
    for i in range(NZ - 1):
        h = h + hr[i].astype(F32)
    u_own = ub[rows(b, TB), :]
    mixed = dot(mix_ref[...], h * jnp.concatenate([u_own, u_own], axis=1),
                precision=lax.Precision.HIGHEST)
    recv("g")
    g = gz[0].astype(F32)
    for i in range(NZ - 1):
        g = g + gr[i].astype(F32)
    ub[0:128, :] = column(ztot[:, rows(b // 2, 128)])
    z_own = ub[rows(b % 2, SB), :]
    student_f = s_raw / snorm
    student_b = student_f.astype(BF16).astype(F32)
    grad_n = (g / jnp.concatenate([z_own, z_own], axis=1) - mixed) / student_temp
    loss = jnp.log(z_own) - jnp.sum(student_b * mixed, axis=1, keepdims=True) / student_temp
    grad_s = (grad_n - student_f * jnp.sum(student_f * grad_n, axis=1, keepdims=True)) / snorm
    out_ref[c, :, 0:D] = grad_s
    out_ref[c, :, D:] = loss
    out_copy = remote(out_ref.at[c], out_ref.at[c], o_ss, o_rs, (dp, 1 - c))
    out_copy.start()

    grad_w = gw[y]
    for o in range(1, NY):
        recv("y%d" % (o - 1))
        grad_w = grad_w + yr[o - 1].astype(F32)
    grad_w = grad_w / student_temp
    weight_f = proto_f / colnorm
    gv_ref[...] = (
        grad_w - weight_f * jnp.sum(weight_f * grad_w, axis=0, keepdims=True)
    ) / colnorm

    wait_bytes(out_ref.at[1 - c], o_rs)
    out_copy.wait_send()
    finish()


def write_out(out_ref, gv_ref, loss_ref, gs_ref, gw_ref):
    gw_ref[...] = gv_ref[...]
    lane = lax.broadcasted_iota(jnp.int32, (IMG, OUTW - D), 1)
    for half in range(2):
        images = slice(half * IMG, (half + 1) * IMG)
        loss = jnp.zeros((IMG, OUTW - D), F32)
        for crop in range(CROPS):
            rows = slice(crop * IMG, (crop + 1) * IMG)
            gs_ref[crop, images, :] = out_ref[half, rows, 0:D]
            loss = jnp.where(lane == crop, out_ref[half, rows, D:], loss)
        loss_ref[images, :] = loss[:, 0:CROPS]


def shards(teacher_feats, student_feats, proto_v):
    mix = mixing()
    mix_big = jnp.asarray(np.kron(np.eye(8, dtype=np.float32), mix), BF16)
    vmem = pl.BlockSpec(memory_space=pltpu.VMEM)
    dma = pltpu.SemaphoreType.DMA
    out, grad_v = pl.pallas_call(
        kernel,
        out_shape=(
            jax.ShapeDtypeStruct((2, SB, OUTW), F32),
            jax.ShapeDtypeStruct((D, PB), F32),
        ),
        in_specs=[pl.BlockSpec(memory_space=pl.ANY)] * 5,
        out_specs=(vmem, vmem),
        scratch_shapes=[
            pltpu.VMEM((2 * IMG, TEACH, D), BF16),
            pltpu.VMEM((CROPS, 2 * IMG, D), BF16),
            pltpu.VMEM((D, PB), BF16),
            pltpu.VMEM((8 * SB, 8 * TB), BF16),
            pltpu.VMEM((SB, TB), F32),
            dma((5,)),
            pltpu.VMEM((NA, D, PB), BF16),
            pltpu.VMEM((TROWS, D), BF16),
            pltpu.VMEM((SROWS, D), BF16),
            pltpu.VMEM((NA, TROWS, PB), F32),
            pltpu.VMEM((NA, TROWS, PB), BF16),
            pltpu.VMEM((NA, SROWS, PB), BF16),
            pltpu.VMEM((D, SROWS), BF16),
            pltpu.VMEM((D, SROWS), BF16),
            pltpu.VMEM((TROWS, 128), F32),
            pltpu.VMEM((NX, ST, D), F32),
            pltpu.VMEM((NX - 1, ST, D), BF16),
            pltpu.VMEM((NX - 1, ST, D), BF16),
            pltpu.VMEM((NZ, SB, D), BF16),
            pltpu.VMEM((NZ - 1, SB, D), BF16),
            pltpu.VMEM((TROWS, D), BF16),
            pltpu.VMEM((NX - 1, NZ * TB, D), BF16),
            pltpu.VMEM((NZ, TB, D), BF16),
            pltpu.VMEM((NZ - 1, TB, D), BF16),
            pltpu.VMEM((NY, D, PB), F32),
            pltpu.VMEM((NY, D, PB), F32),
            pltpu.VMEM((NY, D, PB), F32),
            pltpu.VMEM((NY - 1, D, PB), BF16),
            pltpu.VMEM((NY - 1, D, PB), BF16),
            pltpu.VMEM((SWEEPS, NA, 1, NA * PB), F32),
            pltpu.VMEM((SWEEPS, NB, 1, TROWS), F32),
            pltpu.VMEM((NX - 1, 1, SROWS), F32),
            pltpu.VMEM((NZ - 1, 1, SROWS), F32),
            pltpu.VMEM((1, SROWS), F32),
            pltpu.VMEM((1, SROWS), F32),
            pltpu.VMEM((1, SROWS), F32),
            pltpu.VMEM((TB, D), F32),
            pltpu.VMEM((SB, D), F32),
            pltpu.VMEM((D, TROWS), F32),
            pltpu.VMEM((D, TROWS), F32),
            pltpu.VMEM((NY, TROWS, PB), BF16),
            pltpu.VMEM((2, 1, TROWS), F32),
            dma((2 * NY - 1,)), dma((NA,)),
            dma((NZ - 1,)), dma((NZ - 1,)), dma((NX - 1,)), dma((NX - 1,)),
            dma((NZ - 1,)), dma((NZ - 1,)), dma((NX - 1,)), dma((NX - 1,)),
            dma((NX - 1,)), dma((NX - 1,)),
            dma((SWEEPS,)), dma((SWEEPS,)), dma((SWEEPS,)), dma((SWEEPS,)),
            dma, dma, dma, dma, dma, dma,
            dma((NY,)), dma((NY,)),
            dma((NY - 1,)), dma((NY - 1,)),
            dma, dma,
            dma((NY,)), dma((NY,)),
            dma, dma, dma, dma,
            dma, dma, dma, dma,
        ],
        compiler_params=pltpu.CompilerParams(
            collective_id=0, has_side_effects=True, vmem_limit_bytes=56 << 20
        ),
        name="head_step",
    )(teacher_feats, jnp.transpose(student_feats, (1, 0, 2)), proto_v, mix_big, jnp.asarray(mix))
    loss, grad_s, grad_v = pl.pallas_call(
        write_out,
        out_shape=(
            jax.ShapeDtypeStruct((2 * IMG, CROPS), F32),
            jax.ShapeDtypeStruct((CROPS, 2 * IMG, D), F32),
            jax.ShapeDtypeStruct((D, PB), F32),
        ),
        in_specs=[vmem] * 2,
        out_specs=(vmem,) * 3,
        name="write_out",
    )(out, grad_v)
    return (loss, jnp.transpose(grad_s, (1, 0, 2)), grad_v)


def solution(mesh):
    in_specs = (P("dp", None, None), P("dp", None, None), P(None, ("dp", "proto")))
    out_specs = (P("dp", None), P("dp", None, None), P(None, ("dp", "proto")))
    return jax.shard_map(shards, mesh=mesh, in_specs=in_specs, out_specs=out_specs, check_vma=False)
```

```python
import math

import jax
import jax.numpy as jnp
import numpy as np
from jax import lax
from jax.experimental import pallas as pl
from jax.experimental.pallas import tpu as pltpu
from jax.sharding import PartitionSpec as P

MESH = pl.DeviceIdType.MESH
F32, BF16 = jnp.float32, jnp.bfloat16

epsilon = 1e-12
teacher_temp = 0.07
student_temp = 0.1
LOG2E = math.log2(math.e)

NY, NX, NZ = 4, 4, 8
NB, NA = NX * NZ, NY * 2
D = 256
PB = 256
SB, TB = 64, 16
SROWS, TROWS = SB * NB, TB * NB
IMG, CROPS, TEACH = 6, 10, 2
SWEEPS = 3
ST = SB * NZ
OUTW = D + 128


def mixing():
    m = np.zeros((SB, TB), np.float32)
    for img in range(IMG):
        for crop in range(CROPS):
            row, first = crop * IMG + img, img * TEACH
            if crop == 0:
                m[row, first + 1] = 1.0
            elif crop == 1:
                m[row, first] = 1.0
            else:
                m[row, first] = m[row, first + 1] = 0.5
    return m


def dot(x, y, dims=((1,), (0,)), precision=None):
    return lax.dot_general(x, y, (dims, ((), ())), preferred_element_type=F32, precision=precision)


def wait_bytes(ref, sem):
    pltpu.make_async_copy(ref, ref, sem).wait()


def column(row):
    return jnp.broadcast_to(row, (128, 128)).T


def kernel(t_hbm, s_hbm, p_hbm, mix_big_hbm, mix_hbm, out_ref, gv_ref,
           t_ref, s_ref, p_ref, mix_big_ref, mix_ref, in_sem,
           wg, tg, sg, k3, kv, e3, st_ref, szt, ub, gb, gs, gx, gz, gr, hb, hx, hz, hr, gw, cs, cr, ys, yr,
           colbuf, rowbuf, zx, zbuf, zown, ztmp, ztot, traw, sraw, at, ats, kvs, uu,
           w_ss, w_rs, tz_ss, tz_rs, tx_ss, tx_rs, sz_ss, sz_rs, sx_ss, sx_rs, gx_ss, gx_rs, col_ss, col_rs, row_ss, row_rs, z_ss, z_rs,
           g_ss, g_rs, h_ss, h_rs, c_ss, c_rs, y_ss, y_rs, o_ss, o_rs,
           k_ss, k_rs, at_ss, at_rs, u_ss, u_rs, zx_ss, zx_rs, hx_ss, hx_rs):
    dp = lax.axis_index("dp")
    c = lax.axis_index("proto")
    y, b = dp // NB, dp % NB
    x, zz = b // NZ, b % NZ
    a = y * 2 + c

    def a_dev(a2):
        return ((a2 // 2) * NB + b, a2 % 2)

    def b_dev(b2):
        return (y * NB + b2, c)

    def a_peer(o):
        return (a + o) % NA

    def x_peer(o):
        return (x + o) % NX

    def z_peer(o):
        return (zz + o) % NZ

    def far(i, n):
        return (n // 2 + (2 * (i % 2) - 1) * ((i + 1) // 2)) % n

    def b_far(i):
        return x_peer(far(i % NX, NX)) * NZ + z_peer(far(i // NX, NZ))

    def rows(i, n):
        return pl.ds(pl.multiple_of(i * n, n), n)

    def remote(src, dst, ss, rs, device):
        return pltpu.make_async_remote_copy(
            src_ref=src, dst_ref=dst, send_sem=ss, recv_sem=rs, device_id=device, device_id_type=MESH
        )

    comms = {
        "at": (at, at_ss, at_rs),
        "u": (uu.at[0], u_ss, u_rs),
        "zx": (zx, zx_ss, zx_rs),
        "z": (zbuf, z_ss, z_rs),
        "hx": (hx, hx_ss, hx_rs),
        "g": (gr.at[pl.ds(0, NZ - 1)], g_ss, g_rs),
        "h": (hr, h_ss, h_rs),
    }
    for sweep in range(SWEEPS):
        comms["col%d" % sweep] = (colbuf.at[sweep, pl.ds(0, NA - 1)], col_ss.at[sweep], col_rs.at[sweep])
        comms["row%d" % sweep] = (rowbuf.at[sweep, pl.ds(0, NB - 1)], row_ss.at[sweep], row_rs.at[sweep])
    for z2 in range(1, NZ):
        comms["tz%d" % z2] = (tg.at[pl.ds(0, TB), :], tz_ss.at[z2 - 1], tz_rs.at[z2 - 1])
        comms["sz%d" % z2] = (sg.at[pl.ds(0, SB), :], sz_ss.at[z2 - 1], sz_rs.at[z2 - 1])
    for o in range(1, NX):
        comms["tx%d" % o] = (tg.at[pl.ds(0, NZ * TB), :], tx_ss.at[o - 1], tx_rs.at[o - 1])
        comms["sx%d" % o] = (sg.at[pl.ds(0, NZ * SB), :], sx_ss.at[o - 1], sx_rs.at[o - 1])
        comms["gx%d" % o] = (gx.at[o - 1], gx_ss.at[o - 1], gx_rs.at[o - 1])
    for y2 in range(NY):
        comms["c%d" % y2] = (cs.at[y2], c_ss.at[y2], c_rs.at[y2])
        comms["k%d" % y2] = (kvs.at[y2], k_ss.at[y2], k_rs.at[y2])
    for o in range(NY - 1):
        comms["y%d" % o] = (ys.at[o], y_ss.at[o], y_rs.at[o])
    started, received = [], set()

    def recv(name):
        wait_bytes(comms[name][0], comms[name][2])
        received.add(name)

    def finish():
        for name in started:
            if name not in received:
                recv(name)
            wait_bytes(comms[name][0], comms[name][1])
        for cp in w_copies:
            cp.wait_send()

    barrier = pltpu.get_barrier_semaphore()

    @pl.loop(0, NB - 1)
    def _(i):
        pl.semaphore_signal(barrier, inc=1, device_id=b_dev(b_far(i)), device_id_type=MESH)

    @pl.loop(1, NA)
    def _(o):
        pl.semaphore_signal(barrier, inc=1, device_id=a_dev(a_peer(o)), device_id_type=MESH)

    inputs = [
        pltpu.make_async_copy(src, dst, in_sem.at[n])
        for n, (src, dst) in enumerate([
            (p_hbm, p_ref), (t_hbm, t_ref), (s_hbm, s_ref), (mix_big_hbm, mix_big_ref), (mix_hbm, mix_ref)])
    ]
    for cp in inputs:
        cp.start()
    for cp in inputs:
        cp.wait()

    proto_f = p_ref[...].astype(F32)
    colnorm = jnp.sqrt(jnp.sum(proto_f * proto_f, axis=0, keepdims=True) + epsilon)
    wg[a] = (proto_f / colnorm).astype(BF16)
    traw[...] = jnp.zeros_like(traw)
    for img in range(IMG):
        traw[img * TEACH:(img + 1) * TEACH, :] = t_ref[c * IMG + img].astype(F32)
    t_f = traw[...]
    tg[rows(b, TB), :] = (
        t_f / jnp.sqrt(jnp.sum(t_f * t_f, axis=1, keepdims=True) + epsilon)
    ).astype(BF16)
    sraw[...] = jnp.zeros_like(sraw)
    for crop in range(CROPS):
        both = s_ref[crop].astype(F32)
        sraw[crop * IMG:(crop + 1) * IMG, :] = jnp.where(c == 0, both[:IMG], both[IMG:])
    s_raw = sraw[...]
    snorm = jnp.sqrt(jnp.sum(s_raw * s_raw, axis=1, keepdims=True) + epsilon)
    sg[rows(b, SB), :] = (s_raw / snorm).astype(BF16)

    pl.semaphore_wait(barrier, NA - 1 + NB - 1)

    w_copies = []
    for o in (1, 3, 2):
        cp = remote(wg.at[a], wg.at[a], w_ss.at[o - 1], w_rs.at[a], a_dev(a_peer(2 * o)))
        cp.start()
        w_copies.append(cp)

    def b_all(name, src, dst):
        started.append(name)
        _, ss, rs = comms[name]

        @pl.loop(0, NB - 1)
        def _(i):
            b2 = b_far(i)
            remote(src(b2), dst, ss, rs, b_dev(b2)).start()

    def to_sibling(name, src, dst):
        started.append(name)
        remote(src, dst, comms[name][1], comms[name][2], (dp, 1 - c)).start()

    t_own = tg.at[rows(b, TB), :]
    def t_forward(z2):
        src = tg.at[rows(x * NZ + z2, TB), :]
        for o in (2, 1, 3):
            remote(src, src, tx_ss.at[o - 1], tx_rs.at[o - 1], b_dev(x_peer(o) * NZ + zz)).start()

    for o in (4, 3, 5, 2, 6, 1, 7):
        started.append("tz%d" % o)
        remote(t_own, t_own, tz_ss.at[o - 1], tz_rs.at[o - 1], b_dev(x * NZ + z_peer(o))).start()
    for o in range(1, NX):
        started.append("tx%d" % o)
    t_forward(zz)
    cp = remote(wg.at[a], wg.at[a], w_ss.at[NY - 1], w_rs.at[a], (dp, 1 - c))
    cp.start()
    w_copies.append(cp)
    s_own = sg.at[rows(b, SB), :]

    def s_forward(z2):
        src = sg.at[rows(x * NZ + z2, SB), :]
        for o in range(1, NX):
            remote(src, src, sx_ss.at[o - 1], sx_rs.at[o - 1], b_dev(x_peer(o) * NZ + zz)).start()

    z_order = [1, 7, 2, 6, 3, 5, 4]
    for o in z_order:
        started.append("sz%d" % o)
        remote(s_own, s_own, sz_ss.at[o - 1], sz_rs.at[o - 1], b_dev(x * NZ + z_peer(o))).start()
    for o in range(1, NX):
        started.append("sx%d" % o)
    s_forward(zz)

    for o in (7, 1, 6, 2, 5, 3, 4):
        recv("tz%d" % o)
        t_forward(z_peer(NZ - o))
    for o in (1, 3, 2):
        a2 = a_peer(2 * (NY - o))
        wait_bytes(wg.at[a2], w_rs.at[a2])
        cp = remote(wg.at[a2], wg.at[a2], w_ss.at[NY - 1 + o], w_rs.at[a2], (dp, 1 - c))
        cp.start()
        w_copies.append(cp)
    def s_on(offsets):
        for o in offsets:
            recv("sz%d" % o)
            s_forward(z_peer(NZ - o))

    s_on((7, 1, 6, 2))
    for o in range(1, NX):
        recv("tx%d" % o)
    valid = (lax.broadcasted_iota(jnp.int32, (1, TROWS), 1) % TB < IMG * TEACH).astype(F32)

    def set_u(u_row):
        for r in range(TROWS // 128):
            ub[r * 128:(r + 1) * 128, :] = column(u_row[:, r * 128:(r + 1) * 128])

    set_u(valid)

    def col_send(sweep):
        src = colbuf.at[sweep, a]
        started.append("col%d" % sweep)

        @pl.loop(1, NA)
        def _(o):
            remote(src, src, col_ss.at[sweep], col_rs.at[sweep], a_dev(a_peer(o))).start()

    def col_wait(sweep):
        recv("col%d" % sweep)
        total = colbuf[sweep, 0]
        for i in range(1, NA):
            total = total + colbuf[sweep, i]
        return 1.0 / total

    def row_send(sweep):
        src = rowbuf.at[sweep, b]
        b_all("row%d" % sweep, lambda _: src, src)

    def row_wait(sweep):
        recv("row%d" % sweep)
        total = rowbuf[sweep, 0]
        for i in range(1, NB):
            total = total + rowbuf[sweep, i]
        return valid / total

    def col_part(sweep):
        @pl.loop(0, NA)
        def _(i):
            u2 = ub[...]
            part = jnp.sum(k3[i] * jnp.concatenate([u2, u2], axis=1), axis=0, keepdims=True)
            colbuf[sweep, a, :, rows(i, PB)] = part

    def row_part(sweep, v):
        @pl.loop(0, TROWS // 128)
        def _(r):
            acc = jnp.zeros((128, 128), F32)
            for i in range(NA):
                scaled = k3[i, rows(r, 128), :] * v[:, i * PB:(i + 1) * PB]
                acc = acc + scaled[:, :128] + scaled[:, 128:]
            rowbuf[sweep, b, :, rows(r, 128)] = jnp.sum(acc.T, axis=0, keepdims=True)

    def teacher_grad(v):
        @pl.loop(0, TROWS // 256)
        def _(r):
            h = jnp.zeros((256, D), F32)
            for i in range(NA):
                scaled = (k3[i, rows(r, 256), :] * v[:, i * PB:(i + 1) * PB]).astype(BF16)
                kv[i, rows(r, 256), :] = scaled
                h = h + dot(scaled, wg[i], ((1,), (1,)))
            hb[rows(r, 256), :] = h.astype(BF16)

    def targets(i):
        k = jnp.exp2(dot(tg[...], wg[i]) * (LOG2E / teacher_temp))
        k3[i] = k
        u2 = ub[...]
        colbuf[0, a, :, rows(i, PB)] = jnp.sum(
            k * jnp.concatenate([u2, u2], axis=1), axis=0, keepdims=True)

    def student(step):
        @pl.loop(step, step + 1)
        def _(step):
            r = x_peer(NX - step)
            feats = sg[rows(r, ST), :]
            z = jnp.zeros((ST, 128), F32)
            g = jnp.zeros((ST, D), F32)
            for i in range(NA):
                e = jnp.exp2(dot(feats, wg[i]) * (LOG2E / student_temp))
                z = z + e[:, :128] + e[:, 128:]
                e = e.astype(BF16)
                e3[i, rows(r, ST), :] = e
                g = g + dot(e, wg[i], ((1,), (1,)))
            gb[step] = g
            for j in range(ST // 128):
                part = jnp.sum(z[j * 128:(j + 1) * 128, :].T, axis=0, keepdims=True)
                zown[:, pl.ds(pl.multiple_of(r * ST, ST) + j * 128, 128)] = part
                f_t = feats[j * 128:(j + 1) * 128, :].astype(F32).T
                st_ref[:, pl.ds(pl.multiple_of(r * ST, ST) + j * 128, 128)] = f_t.astype(BF16)

    def student_send(step):
        if step:
            o = NX - step
            gs[step - 1] = gb[step].astype(BF16)
            started.append("gx%d" % o)
            remote(gs.at[step - 1], gx.at[o - 1], gx_ss.at[o - 1], gx_rs.at[o - 1],
                   b_dev(x_peer(o) * NZ + zz)).start()

    def student_step(step):
        if step:
            recv("sx%d" % step)
        student(step)

    targets(a)
    for o in range(1, NY):
        targets(a_peer(2 * (NY - o)))
    for o in (0, 3, 1, 2):
        a2 = ((y + o) % NY) * 2 + 1 - c
        wait_bytes(wg.at[a2], w_rs.at[a2])
        targets(a2)
    col_send(0)
    s_on((5, 3, 4))
    student_step(0)
    v = col_wait(0)
    row_part(0, v)
    row_send(0)
    student_step(1)
    student_step(3)
    set_u(row_wait(0))
    col_part(1)
    col_send(1)
    student_send(1)
    student_send(3)
    student_step(2)
    started.append("zx")
    for o in range(1, NX):
        remote(zown, zx.at[o - 1], zx_ss, zx_rs, b_dev(x_peer(o) * NZ + zz)).start()
    v = col_wait(1)
    row_part(1, v)
    row_send(1)
    recv("zx")
    ztmp[...] = zown[...] + zx[0] + zx[1] + zx[2]
    started.append("z")
    for o in z_order:
        remote(ztmp, zbuf.at[o - 1], z_ss, z_rs, b_dev(x * NZ + z_peer(o))).start()
    set_u(row_wait(1))
    col_part(2)
    col_send(2)
    student_send(2)
    for j in range(TROWS // 128):
        at[:, j * 128:(j + 1) * 128] = dot(st_ref[:, j * 512:(j + 1) * 512], mix_big_ref[...])
    to_sibling("at", at, ats)
    recv("z")
    zsum = ztmp[...]
    for i in range(NZ - 1):
        zsum = zsum + zbuf[i]
    ztot[...] = zsum
    z_inv = 1.0 / zsum
    for j in range(SROWS // 512):
        szt[:, j * 512:(j + 1) * 512] = (
            st_ref[:, j * 512:(j + 1) * 512].astype(F32) * z_inv[:, j * 512:(j + 1) * 512]
        ).astype(BF16)
    for y2 in range(NY):
        cs[y2] = dot(szt[...], e3[y2 * 2 + 1 - c])
        to_sibling("c%d" % y2, cs.at[y2], cr.at[y2])
    for y2 in range(NY):
        gw[y2] = dot(szt[...], e3[y2 * 2 + c])
    v = col_wait(2)
    row_part(2, v)
    row_send(2)
    teacher_grad(v)
    started.append("hx")
    for o in range(1, NX):
        remote(hb.at[rows(x_peer(o), NZ * TB), :], hx.at[o - 1], hx_ss, hx_rs,
               b_dev(x_peer(o) * NZ + zz)).start()
    for y2 in range(NY):
        to_sibling("k%d" % y2, kv.at[y2 * 2 + 1 - c], kvs.at[y2])
    for o in range(1, NX):
        recv("gx%d" % o)
    started.append("g")
    for o in z_order + [0]:
        z2 = z_peer(o)
        g = gb[0, rows(z2, SB), :]
        for i in range(NX - 1):
            g = g + gx[i, rows(z2, SB), :].astype(F32)
        gz[o] = g.astype(BF16)
        if o:
            remote(gz.at[o], gr.at[o - 1], g_ss, g_rs, b_dev(x * NZ + z2)).start()
    u_row = row_wait(2)
    uu[c] = u_row
    to_sibling("u", uu.at[c], uu.at[c])
    set_u(u_row)

    def scaled_mix(mixed_t, u2):
        full = mixed_t * u2
        high = full.astype(BF16)
        return jnp.concatenate([high, (full - high.astype(F32)).astype(BF16)], axis=0)

    def teacher_part(ua, k2):
        both = dot(ua, k2)
        return both[:D] + both[D:]

    ua = scaled_mix(at[...], u_row)
    for y2 in range(NY):
        gw[y2] = gw[y2] - teacher_part(ua, kv[y2 * 2 + c])
    recv("at")
    recv("u")
    ua = scaled_mix(ats[...], uu[1 - c])
    for name in range(NY):
        recv("k%d" % name)
        recv("c%d" % name)
    for o in (2, 1, 3, 0):
        y2 = (y + o) % NY
        both = gw[y2] + cr[y2] - teacher_part(ua, kvs[y2])
        if o:
            ys[o - 1] = both.astype(BF16)
            started.append("y%d" % (o - 1))
            remote(ys.at[o - 1], yr.at[o - 1], y_ss.at[o - 1], y_rs.at[o - 1],
                   (y2 * NB + b, c)).start()
        else:
            gw[y2] = both

    recv("hx")
    started.append("h")
    for o in z_order + [0]:
        z2 = z_peer(o)
        h = hb[rows(x * NZ + z2, TB), :].astype(F32)
        for i in range(NX - 1):
            h = h + hx[i, rows(z2, TB), :].astype(F32)
        hz[o] = h.astype(BF16)
        if o:
            remote(hz.at[o], hr.at[o - 1], h_ss, h_rs, b_dev(x * NZ + z2)).start()

    recv("g")
    g = gz[0].astype(F32)
    for i in range(NZ - 1):
        g = g + gr[i].astype(F32)
    u_own = ub[rows(b, TB), :]
    u_own = jnp.concatenate([u_own, u_own], axis=1)
    ub[0:128, :] = column(ztot[:, rows(b // 2, 128)])
    z_own = ub[rows(b % 2, SB), :]
    g = g / jnp.concatenate([z_own, z_own], axis=1)
    recv("h")
    h = hz[0].astype(F32)
    for i in range(NZ - 1):
        h = h + hr[i].astype(F32)
    mixed = dot(mix_ref[...], h * u_own, precision=lax.Precision.HIGHEST)
    student_f = s_raw / snorm
    student_b = student_f.astype(BF16).astype(F32)
    grad_n = (g - mixed) / student_temp
    loss = jnp.log(z_own) - jnp.sum(student_b * mixed, axis=1, keepdims=True) / student_temp
    grad_s = (grad_n - student_f * jnp.sum(student_f * grad_n, axis=1, keepdims=True)) / snorm
    out_ref[c, :, 0:D] = grad_s
    out_ref[c, :, D:] = loss
    out_copy = remote(out_ref.at[c], out_ref.at[c], o_ss, o_rs, (dp, 1 - c))
    out_copy.start()

    grad_w = gw[y]
    for o in range(1, NY):
        recv("y%d" % (o - 1))
        grad_w = grad_w + yr[o - 1].astype(F32)
    grad_w = grad_w / student_temp
    weight_f = proto_f / colnorm
    gv_ref[...] = (
        grad_w - weight_f * jnp.sum(weight_f * grad_w, axis=0, keepdims=True)
    ) / colnorm

    wait_bytes(out_ref.at[1 - c], o_rs)
    out_copy.wait_send()
    finish()


def write_out(out_ref, gv_ref, loss_ref, gs_ref, gw_ref):
    gw_ref[...] = gv_ref[...]
    lane = lax.broadcasted_iota(jnp.int32, (IMG, OUTW - D), 1)
    for half in range(2):
        images = slice(half * IMG, (half + 1) * IMG)
        loss = jnp.zeros((IMG, OUTW - D), F32)
        for crop in range(CROPS):
            rows = slice(crop * IMG, (crop + 1) * IMG)
            gs_ref[crop, images, :] = out_ref[half, rows, 0:D]
            loss = jnp.where(lane == crop, out_ref[half, rows, D:], loss)
        loss_ref[images, :] = loss[:, 0:CROPS]


def shards(teacher_feats, student_feats, proto_v):
    mix = mixing()
    mix_big = jnp.asarray(np.kron(np.eye(8, dtype=np.float32), mix), BF16)
    vmem = pl.BlockSpec(memory_space=pltpu.VMEM)
    dma = pltpu.SemaphoreType.DMA
    out, grad_v = pl.pallas_call(
        kernel,
        out_shape=(
            jax.ShapeDtypeStruct((2, SB, OUTW), F32),
            jax.ShapeDtypeStruct((D, PB), F32),
        ),
        in_specs=[pl.BlockSpec(memory_space=pl.ANY)] * 5,
        out_specs=(vmem, vmem),
        scratch_shapes=[
            pltpu.VMEM((2 * IMG, TEACH, D), BF16),
            pltpu.VMEM((CROPS, 2 * IMG, D), BF16),
            pltpu.VMEM((D, PB), BF16),
            pltpu.VMEM((8 * SB, 8 * TB), BF16),
            pltpu.VMEM((SB, TB), F32),
            dma((5,)),
            pltpu.VMEM((NA, D, PB), BF16),
            pltpu.VMEM((TROWS, D), BF16),
            pltpu.VMEM((SROWS, D), BF16),
            pltpu.VMEM((NA, TROWS, PB), F32),
            pltpu.VMEM((NA, TROWS, PB), BF16),
            pltpu.VMEM((NA, SROWS, PB), BF16),
            pltpu.VMEM((D, SROWS), BF16),
            pltpu.VMEM((D, SROWS), BF16),
            pltpu.VMEM((TROWS, 128), F32),
            pltpu.VMEM((NX, ST, D), F32),
            pltpu.VMEM((NX - 1, ST, D), BF16),
            pltpu.VMEM((NX - 1, ST, D), BF16),
            pltpu.VMEM((NZ, SB, D), BF16),
            pltpu.VMEM((NZ - 1, SB, D), BF16),
            pltpu.VMEM((TROWS, D), BF16),
            pltpu.VMEM((NX - 1, NZ * TB, D), BF16),
            pltpu.VMEM((NZ, TB, D), BF16),
            pltpu.VMEM((NZ - 1, TB, D), BF16),
            pltpu.VMEM((NY, D, PB), F32),
            pltpu.VMEM((NY, D, PB), F32),
            pltpu.VMEM((NY, D, PB), F32),
            pltpu.VMEM((NY - 1, D, PB), BF16),
            pltpu.VMEM((NY - 1, D, PB), BF16),
            pltpu.VMEM((SWEEPS, NA, 1, NA * PB), F32),
            pltpu.VMEM((SWEEPS, NB, 1, TROWS), F32),
            pltpu.VMEM((NX - 1, 1, SROWS), F32),
            pltpu.VMEM((NZ - 1, 1, SROWS), F32),
            pltpu.VMEM((1, SROWS), F32),
            pltpu.VMEM((1, SROWS), F32),
            pltpu.VMEM((1, SROWS), F32),
            pltpu.VMEM((TB, D), F32),
            pltpu.VMEM((SB, D), F32),
            pltpu.VMEM((D, TROWS), F32),
            pltpu.VMEM((D, TROWS), F32),
            pltpu.VMEM((NY, TROWS, PB), BF16),
            pltpu.VMEM((2, 1, TROWS), F32),
            dma((2 * NY - 1,)), dma((NA,)),
            dma((NZ - 1,)), dma((NZ - 1,)), dma((NX - 1,)), dma((NX - 1,)),
            dma((NZ - 1,)), dma((NZ - 1,)), dma((NX - 1,)), dma((NX - 1,)),
            dma((NX - 1,)), dma((NX - 1,)),
            dma((SWEEPS,)), dma((SWEEPS,)), dma((SWEEPS,)), dma((SWEEPS,)),
            dma, dma, dma, dma, dma, dma,
            dma((NY,)), dma((NY,)),
            dma((NY - 1,)), dma((NY - 1,)),
            dma, dma,
            dma((NY,)), dma((NY,)),
            dma, dma, dma, dma,
            dma, dma, dma, dma,
        ],
        compiler_params=pltpu.CompilerParams(
            collective_id=0, has_side_effects=True, vmem_limit_bytes=56 << 20
        ),
        name="head_step",
    )(teacher_feats, jnp.transpose(student_feats, (1, 0, 2)), proto_v, mix_big, jnp.asarray(mix))
    loss, grad_s, grad_v = pl.pallas_call(
        write_out,
        out_shape=(
            jax.ShapeDtypeStruct((2 * IMG, CROPS), F32),
            jax.ShapeDtypeStruct((CROPS, 2 * IMG, D), F32),
            jax.ShapeDtypeStruct((D, PB), F32),
        ),
        in_specs=[vmem] * 2,
        out_specs=(vmem,) * 3,
        name="write_out",
    )(out, grad_v)
    return (loss, jnp.transpose(grad_s, (1, 0, 2)), grad_v)


def solution(mesh):
    in_specs = (P("dp", None, None), P("dp", None, None), P(None, ("dp", "proto")))
    out_specs = (P("dp", None), P("dp", None, None), P(None, ("dp", "proto")))
    return jax.shard_map(shards, mesh=mesh, in_specs=in_specs, out_specs=out_specs, check_vma=False)
```
